256 devices in a mesh: cells: 64 (over z, y, core), cols: 4 (over x).
Axes of the slice: x: 4, y: 4, z: 8, core: 2. Of those that a mesh axis runs over, the one named last changes fastest.
Arguments:
- start_block: float32 [64, 98304], P('cols', 'cells')
- stiffness: float32 [343, 343], replicated
- cell_scale: float32 [4096], P('cells'), may hold values from 0.25 to 2
- node_weight: float32 [343, 4096], P(None, 'cells'), may hold values from -0.25 to 0.75
- cell_count: int32 [64], P('cells'), may hold values from 8 to 64, as said below
- conn: int32 [343, 4096], P(None, 'cells'), may hold values from 0 to 2047, as said below
- send_rows: int32 [128, 256], P('cells'), may hold values from 0 to 1535, as said below
- filter_bounds: float32 [2], replicated, may hold values from 1.2 to 1.6
Outputs:
- filtered: float32 [64, 98304], P('cols', 'cells')
- correlation: float32 [64, 64], P('cells', 'cols')
- projected: float32 [64, 64], P('cells', 'cols')
The draws below stay inside these ranges and needn't reach their ends.
Inputs may be any that keep to these rules, and one draw needn't show every extreme that they name: `cell_count`: each partition has at least 8 live cells; some partition has exactly 64, some exactly 8. `conn`: entries index the extended rows of the slot's own partition: below 1536 its own nodes, then 256 copies from the left neighbour, then 256 from the right. `send_rows`: for partition p, the list for the left neighbour (row 2p) holds 256 distinct rows of partition p below 768, and the list for the right neighbour (row 2p + 1) holds 256 distinct rows of partition p from 768 on.
All inputs are finite; a program needn't handle non-finite values.
Results may differ from the reference program's by a relative error of at most 0.00025.
Values sent between devices are 32-bit elements; how exact they have to be, the bound alone decides.
A program may use at most 64 MiB of HBM per device.

```python
import math
import jax
import jax.numpy as jnp
from jax import lax

BLOCK = 64
NPC = 343
NODE_DEV = 1536
GHOST = 256
CELL_CAP = 64
DEGREE = 4
MULT = 10
PARTITIONS = 64
NODES = 98304
CELLS = 4096


def draw_start_block(key, part):
    key = jax.random.fold_in(key, 11)
    first = jax.random.fold_in(key, 0)
    ramp = 0.6 + 1.2 * jnp.arange(NODES, dtype=jnp.float32) / NODES
    base = jax.random.normal(first, (BLOCK, NODES), jnp.float32)
    return base * ramp[None, :]


def draw_stiffness(key, part):
    key = jax.random.fold_in(key, 12)
    noise = jax.random.uniform(key, (NPC, NPC), jnp.float32, -0.02, 0.02)
    rows = jnp.arange(NPC)[:, None]
    cols = jnp.arange(NPC)[None, :]
    eye = (rows == cols).astype(jnp.float32)
    return noise + noise.T + eye


def draw_cell_count(key, part):
    key = jax.random.fold_in(key, 13)
    keys = jax.random.split(key, 5)
    light = jax.random.randint(keys[0], (PARTITIONS,), CELL_CAP // 8, CELL_CAP // 2 + 1)
    heavy = jax.random.randint(keys[1], (PARTITIONS,), 3 * CELL_CAP // 4, CELL_CAP + 1)
    pick = jax.random.randint(keys[2], (PARTITIONS,), 0, 4) == 0
    count = jnp.where(pick, heavy, light)
    top = jax.random.randint(keys[3], (), 0, PARTITIONS)
    low = (top + 1 + jax.random.randint(keys[4], (), 0, PARTITIONS - 1)) % PARTITIONS
    index = jnp.arange(PARTITIONS)
    count = jnp.where(index == top, CELL_CAP, count)
    count = jnp.where(index == low, CELL_CAP // 8, count)
    return count.astype(jnp.int32)


def draw_conn(key, part):
    key = jax.random.fold_in(key, 14)
    links = jax.random.randint(key, (NPC, CELLS), 0, NODE_DEV + 2 * GHOST)
    links = links.at[0, 0].set(NODE_DEV + 2 * GHOST - 1)
    links = links.at[1, 0].set(0)
    return links.astype(jnp.int32)


def draw_send_rows(key, part):
    key = jax.random.fold_in(key, 15)
    half = NODE_DEV // 2
    keys = jax.random.split(key, 2 * PARTITIONS)
    rows = jax.vmap(lambda k: jax.random.permutation(k, half)[:GHOST])(keys).astype(jnp.int32)
    offset = jnp.arange(2 * PARTITIONS, dtype=jnp.int32) % 2 * half
    return rows + offset[:, None]


def steps_of(key, shape, shards, low, top_value):
    level, own = 1.0, jax.random.fold_in(key, 6)
    for position, parts in shards:
        steps = jnp.exp(jax.random.uniform(jax.random.fold_in(own, position), (parts,), jnp.float32, low / len(shards), top_value / len(shards)))
        level = level * jnp.repeat(steps, shape[position] // parts).reshape([-1 if axis == position else 1 for axis in range(len(shape))])
    return level


def setup_inputs(seed: int = 0) -> dict:
    splits = jax.random.split(jax.random.key(seed), 9)
    start_block = draw_start_block(jax.random.fold_in(splits[8], 71), 0)
    stiffness = draw_stiffness(jax.random.fold_in(splits[8], 71), 0)
    cell_scale = jnp.clip(jnp.exp(math.log(2.0) - 2.0794415 * jax.random.uniform(splits[2], (CELLS,), jnp.float32) ** steps_of(splits[2], (CELLS,), ((0, 64),), -0.2, 0.2)), 0.25, 2.0)
    node_weight = jnp.clip(-0.25 + 1.0 * jax.random.uniform(splits[3], (NPC, CELLS), jnp.float32) ** steps_of(splits[3], (NPC, CELLS), ((1, 64),), -0.2, 0.2), -0.25, 0.75)
    cell_count = draw_cell_count(jax.random.fold_in(splits[8], 71), 0)
    conn = draw_conn(jax.random.fold_in(splits[8], 71), 0)
    send_rows = draw_send_rows(jax.random.fold_in(splits[8], 71), 0)
    filter_bounds = jnp.clip(jax.random.uniform(splits[7], (2,), jnp.float32, 1.2, 1.6), 1.2, 1.6)
    return dict(start_block=start_block, stiffness=stiffness, cell_scale=cell_scale, node_weight=node_weight, cell_count=cell_count, conn=conn, send_rows=send_rows, filter_bounds=filter_bounds)


def cell_terms(extended, links, scale, weight, alive, stiffness):
    local = extended[:, links]
    spread = jnp.einsum("ij,bjc->bic", stiffness, local, precision=lax.Precision.HIGHEST)
    terms = (spread * scale[None, None, :] + local * weight[None, :, :]) * (alive[None, None, :] / MULT)
    return jnp.zeros(extended.shape, jnp.float32).at[:, links].add(terms)


def apply_operator(vec, stiffness, cell_scale, node_weight, cell_count, conn, send_rows):
    blocks = vec.reshape(BLOCK, PARTITIONS, NODE_DEV).transpose(1, 0, 2)
    sends = send_rows.reshape(PARTITIONS, 2, GHOST)
    take = jax.vmap(lambda b, s: b[:, s])
    to_left = take(blocks, sends[:, 0])
    to_right = take(blocks, sends[:, 1])
    zero = jnp.zeros((1, BLOCK, GHOST), jnp.float32)
    from_left = jnp.concatenate([zero, to_right[:-1]], 0)
    from_right = jnp.concatenate([to_left[1:], zero], 0)
    extended = jnp.concatenate([blocks, from_left, from_right], 2)
    links = conn.reshape(NPC, PARTITIONS, CELL_CAP).transpose(1, 0, 2)
    scales = cell_scale.reshape(PARTITIONS, CELL_CAP)
    weights = node_weight.reshape(NPC, PARTITIONS, CELL_CAP).transpose(1, 0, 2)
    slots = jnp.arange(CELL_CAP, dtype=jnp.int32)
    alive = (slots[None, :] < cell_count[:, None]).astype(jnp.float32)

    def one_part(items):
        return cell_terms(items[0], items[1], items[2], items[3], items[4], stiffness)

    pieces = lax.map(one_part, (extended, links, scales, weights, alive))
    owned = pieces[:, :, :NODE_DEV]
    back_left = pieces[:, :, NODE_DEV:NODE_DEV + GHOST]
    back_right = pieces[:, :, NODE_DEV + GHOST:]
    add_right = jnp.concatenate([back_left[1:], zero], 0)
    add_left = jnp.concatenate([zero, back_right[:-1]], 0)
    scatter = jax.vmap(lambda o, s, a: o.at[:, s].add(a))
    owned = scatter(owned, sends[:, 1], add_right)
    owned = scatter(owned, sends[:, 0], add_left)
    return owned.transpose(1, 0, 2).reshape(BLOCK, NODES)


def reference(start_block, stiffness, cell_scale, node_weight, cell_count, conn, send_rows, filter_bounds):
    center = filter_bounds[0]
    half = filter_bounds[1]

    def operator(vec):
        return apply_operator(vec, stiffness, cell_scale, node_weight, cell_count, conn, send_rows)

    previous = start_block
    current = (operator(previous) - center * previous) / half
    for step in range(DEGREE - 1):
        following = 2.0 * ((operator(current) - center * current) / half) - previous
        previous = current
        current = following
    image = operator(current)
    correlation = jnp.dot(current, current.T, precision=lax.Precision.HIGHEST) / NODES
    projected = jnp.dot(current, image.T, precision=lax.Precision.HIGHEST) / NODES
    return current, correlation, projected
```

```python
import functools

import jax
import jax.numpy as jnp
from jax import lax
from jax.experimental import pallas as pl
from jax.experimental.pallas import tpu as pltpu
from jax.sharding import PartitionSpec as P

DEGREE = 4
MULT = 10
LANES = 128
CHUNK = 8
BF16 = jnp.bfloat16
F32 = jnp.float32
I32 = jnp.int32
MESH = pl.DeviceIdType.MESH


def iota(shape, dim):
    return lax.broadcasted_iota(I32, shape, dim)


def split(x):
    high = x.astype(BF16)
    return high, (x - high.astype(F32)).astype(BF16)


def dot(a, b):
    return jnp.dot(a, b, preferred_element_type=F32)


def dot_nt(a, b):
    return lax.dot_general(a, b, (((1,), (1,)), ((), ())), preferred_element_type=F32)


def pick(x, index):
    return jnp.take_along_axis(x, index, axis=1, mode="promise_in_bounds")


def mark(condition):
    return jnp.where(condition, 1.0, 0.0).astype(F32)


def kernel(
    cfg,
    start,
    stiff,
    scale,
    weight,
    count,
    conn,
    send,
    bounds,
    out_filtered,
    out_corr,
    out_proj,
    kpad,
    kk,
    ci,
    newc,
    newr,
    tab,
    rows_nm,
    wt,
    sc,
    onehot,
    masks,
    vcur,
    vprev,
    image,
    xa,
    xb,
    amat,
    acc,
    part,
    from_left,
    from_right,
    gath,
    gsum,
    got1,
    mid,
    got2,
    ssem,
    rsem,
    gssem,
    grsem,
    s1sem,
    r1sem,
    s2sem,
    r2sem,
):
    width, owned, ghost, npc, cells, parts, cols, inner = cfg
    slots = kk.shape[0]
    groups = (owned + 2 * ghost) // ghost
    half = groups * width
    tiles = 2 * groups
    near = inner
    far = parts // inner

    p = lax.axis_index("cells")
    q = lax.axis_index("cols")
    left = lax.rem(p + parts - 1, parts)
    right = lax.rem(p + 1, parts)
    z = lax.div(p, near)
    yc = lax.rem(p, near)

    far_peers = [lax.rem(z + d, far) * near + yc for d in range(1, far)]
    near_peers = [z * near + lax.rem(yc + d, near) for d in range(1, near)]
    col_peers = [lax.rem(q + d, cols) for d in range(1, cols)]

    barrier = pltpu.get_barrier_semaphore()
    targets = [(left, q), (right, q)]
    targets += [(p, other) for other in col_peers]
    targets += [(other, q) for other in far_peers]
    targets += [(other, q) for other in near_peers]
    for target in targets:
        pl.semaphore_signal(barrier, inc=1, device_id=target, device_id_type=MESH)

    kpad[...] = jnp.zeros_like(kpad)
    kpad[0:npc, 0:npc] = stiff[...]
    k_high, k_low = split(kpad[...].T)
    kk[:, 0:slots] = k_high
    kk[:, slots:] = k_low

    lane = iota((1, LANES), 1)
    per_side = owned // 2 // LANES
    rows_nm[...] = jnp.zeros_like(rows_nm)
    places = []
    for side in range(2):
        column = jnp.broadcast_to(send[side : side + 1, :].astype(F32), (LANES, ghost)).T
        order = (iota((ghost, LANES), 0) + 1).astype(F32)
        for t in range(per_side):
            tile = side * per_side + t
            here = (iota((ghost, LANES), 1) + tile * LANES).astype(F32)
            place = jnp.sum(jnp.where(column == here, order, 0.0), axis=0, keepdims=True)
            places.append(place)
            rows_nm[tile : tile + 1, :] = mark(place == 0.0)
    free = rows_nm[...].astype(BF16)
    before = mark(iota((LANES, LANES), 0) < iota((LANES, LANES), 1)).astype(BF16)
    above = mark(iota((LANES, LANES), 0) > iota((LANES, LANES), 1)).astype(BF16)
    ones = jnp.ones((LANES, LANES), BF16)
    rank = dot(free, before) + dot(above, dot(free, ones).astype(BF16))
    base = (ghost, owned)
    for tile in range(2 * per_side):
        place = places[tile]
        shared = place + float(base[tile // per_side] - 1)
        inside = rank[tile : tile + 1, :] + float(2 * ghost)
        tab[tile : tile + 1, :] = jnp.where(place > 0.0, shared, inside).astype(I32)
    for t in range(ghost // LANES):
        a = 2 * per_side + t
        b = a + ghost // LANES
        tab[a : a + 1, :] = lane + t * LANES
        tab[b : b + 1, :] = lane + (owned + ghost + t * LANES)

    ci[...] = jnp.zeros_like(ci)
    ci[0:npc, 0:cells] = conn[...]
    block = 64

    @pl.loop(0, slots // block)
    def _(i):
        rows = pl.ds(pl.multiple_of(i * block, block), block)
        index = ci[rows, :]
        low = index & (LANES - 1)
        tile = index >> 7
        value = None
        for t in range(tiles):
            got = pick(jnp.broadcast_to(tab[t : t + 1, :], (block, LANES)), low)
            value = got if value is None else jnp.where(tile == t, got, value)
        newc[rows, :] = value

    newr[...] = newc[...].astype(F32).T.astype(I32)

    live = mark(iota((LANES, slots), 0) < count[0, 0]) * (1.0 / MULT)
    kpad[:, 0:LANES] = jnp.zeros((slots, LANES), F32)
    kpad[0:npc, 0:cells] = weight[...]
    wt[...] = kpad[:, 0:LANES].T * live
    scale_row = jnp.concatenate([scale[...], jnp.zeros((1, LANES - cells), F32)], axis=1)
    scale_col = jnp.broadcast_to(scale_row, (LANES, LANES)).T
    sc[...] = jnp.concatenate([scale_col] * (slots // LANES), axis=1) * live

    @pl.loop(0, cells)
    def _(c):
        column = pick(newc[...] & (ghost - 1), jnp.full((slots, LANES), c, I32))
        rows = pl.ds(pl.multiple_of(c * slots, slots), slots)
        for t in range(ghost // LANES):
            hit = mark(column == iota((slots, LANES), 1) + t * LANES)
            onehot[rows, t * LANES : (t + 1) * LANES] = hit.astype(BF16)
        group = jnp.broadcast_to(newr[pl.ds(c, 1), :] >> 8, (half, slots))
        member = mark(group == iota((half, slots), 0) // width)
        masks[pl.ds(pl.multiple_of(c * half, half), half), :] = member.astype(BF16)

    tab_cols = jnp.concatenate([tab[...], jnp.zeros((LANES - tiles, LANES), I32)], axis=0).astype(F32).T.astype(I32)
    total = jnp.zeros((2 * half, ghost), F32)
    for t in range(owned // LANES):
        high, low = split(start[:, t * LANES : (t + 1) * LANES])
        group = jnp.broadcast_to(tab[t : t + 1, :] >> 8, (half, LANES))
        member = mark(group == iota((half, LANES), 0) // width).astype(BF16)
        left_side = jnp.concatenate(
            [jnp.concatenate([high] * groups, axis=0) * member, jnp.concatenate([low] * groups, axis=0) * member], axis=0
        )
        column = jnp.broadcast_to(tab_cols[:, t : t + 1] & (ghost - 1), (LANES, ghost))
        total += dot(left_side, mark(column == iota((LANES, ghost), 1)).astype(BF16))
    part[0] = total[0:half] + total[half:]

    pl.semaphore_wait(barrier, len(targets))

    has_left = jnp.where(p > 0, 1.0, 0.0).astype(F32)
    has_right = jnp.where(p < parts - 1, 1.0, 0.0).astype(F32)
    pair = 2 * width

    def exchange(step):
        to_left = pltpu.make_async_remote_copy(
            src_ref=part.at[step, pl.ds(0, pair)],
            dst_ref=from_right.at[step],
            send_sem=ssem.at[0, step],
            recv_sem=rsem.at[0, step],
            device_id=(left, q),
            device_id_type=MESH,
        )
        to_right = pltpu.make_async_remote_copy(
            src_ref=part.at[step, pl.ds(half - pair, pair)],
            dst_ref=from_left.at[step],
            send_sem=ssem.at[1, step],
            recv_sem=rsem.at[1, step],
            device_id=(right, q),
            device_id_type=MESH,
        )
        to_left.start()
        to_right.start()
        to_left.wait()
        to_right.wait()
        a = part[step, 0:width, :] + from_left[step, 0:width, :]
        b = part[step, width:pair, :] + from_left[step, width:pair, :] * has_left
        c = part[step, half - pair : half - width, :] + from_right[step, 0:width, :] * has_right
        d = part[step, half - width : half, :] + from_right[step, width:pair, :]
        return jnp.concatenate([a * has_left, b, part[step, pair : half - pair, :], c, d * has_right], axis=0)

    def gather(chunk, dest):
        for c in range(CHUNK):
            row = newr[pl.ds(chunk * CHUNK + c, 1), :]
            for l in range(slots // LANES):
                index = jnp.broadcast_to(row[:, l * LANES : (l + 1) * LANES], (width, LANES))
                low = index & (LANES - 1)
                tile = index >> 7
                value = None
                for t in range(tiles):
                    source = vcur[(t // 2) * width : (t // 2 + 1) * width, (t % 2) * LANES : (t % 2 + 1) * LANES]
                    got = pick(source, low)
                    value = got if value is None else jnp.where(tile == t, got, value)
                dest[c * width : (c + 1) * width, l * LANES : (l + 1) * LANES] = value

    def process(chunk, x):
        high, low = split(x[...])
        wide = dot(high, kk[...])
        spread = wide[:, 0:slots] + wide[:, slots:] + dot(low, kk[:, 0:slots])
        for c in range(CHUNK):
            cell = chunk * CHUNK + c
            rows = slice(c * width, (c + 1) * width)
            term = spread[rows] * sc[pl.ds(cell, 1), :] + x[rows, :] * wt[pl.ds(cell, 1), :]
            high, low = split(term)
            for g in range(groups):
                member = masks[pl.ds(pl.multiple_of(cell * half + g * width, width), width), :]
                amat[g * width : (g + 1) * width, c * slots : (c + 1) * slots] = high * member
                amat[half + g * width : half + (g + 1) * width, c * slots : (c + 1) * slots] = low * member
        span = CHUNK * slots
        acc[...] += dot(amat[...], onehot[pl.ds(pl.multiple_of(chunk * span, span), span), :])

    def gather_copy(d):
        return pltpu.make_async_remote_copy(
            src_ref=gath.at[0],
            dst_ref=gath.at[d],
            send_sem=gssem.at[d],
            recv_sem=grsem.at[d],
            device_id=(p, col_peers[d - 1]),
            device_id_type=MESH,
        )

    vcur[...] = exchange(0)
    vprev[...] = jnp.zeros_like(vprev)
    center = bounds[0, 0]
    inverse = 1.0 / jnp.full((1, ghost), bounds[0, 1], F32)
    chunks = cells // CHUNK

    @pl.loop(1, DEGREE + 2)
    def _(step):
        acc[...] = jnp.zeros_like(acc)
        gather(0, xa)

        @pl.loop(0, chunks // 2)
        def _(i):
            gather(2 * i + 1, xb)
            process(2 * i, xa)
            gather(lax.rem(2 * i + 2, chunks), xa)
            process(2 * i + 1, xb)

        part[step] = acc[0:half, :] + acc[half:, :]
        applied = exchange(step)
        image[...] = applied

        @pl.when(step <= DEGREE)
        def _():
            current = vcur[...]
            factor = inverse * jnp.where(step > 1, 2.0, 1.0).astype(F32)
            following = (applied - center * current) * factor - vprev[...]
            vprev[...] = current
            vcur[...] = following

        @pl.when(step == DEGREE)
        def _():
            gath[0] = vcur[width : half - width, :]
            for d in range(1, cols):
                gather_copy(d).start()

    for t in range(owned // LANES):
        index = jnp.broadcast_to(tab[t : t + 1, :], (width, LANES))
        low = index & (LANES - 1)
        tile = index >> 7
        value = None
        for s in range(2, tiles - 2):
            source = vcur[(s // 2) * width : (s // 2 + 1) * width, (s % 2) * LANES : (s % 2 + 1) * LANES]
            got = pick(source, low)
            value = got if value is None else jnp.where(tile == s, got, value)
        out_filtered[:, t * LANES : (t + 1) * LANES] = value

    for d in range(1, cols):
        gather_copy(d).wait()

    gram = [jnp.zeros((width, 2 * width), F32) for _ in range(cols)]
    for g in range(groups - 2):
        rows = slice(g * width, (g + 1) * width)
        mine = jnp.concatenate([gath[0, rows, :], image[(g + 1) * width : (g + 2) * width, :]], axis=0)
        all_rows = jnp.concatenate([gath[d, rows, :] for d in range(cols)], axis=0)
        mine_high, mine_low = split(mine)
        all_high, all_low = split(all_rows)
        term = dot_nt(all_high, mine_high) + dot_nt(all_high, mine_low) + dot_nt(all_low, mine_high)
        gram = [gram[d] + term[d * width : (d + 1) * width] for d in range(cols)]
    gsum[...] = jnp.zeros_like(gsum)
    for d in range(cols):
        group = lax.rem(q + cols - d, cols)
        gsum[pl.ds(pl.multiple_of(group * width, width), width), 0 : 2 * width] = gram[d] * (1.0 / (parts * owned))

    def far_copy(d):
        block = lax.rem(z + d, far) * near
        return pltpu.make_async_remote_copy(
            src_ref=gsum.at[pl.ds(pl.multiple_of(block, near), near)],
            dst_ref=got1.at[d],
            send_sem=s1sem.at[d],
            recv_sem=r1sem.at[d],
            device_id=(far_peers[d - 1], q),
            device_id_type=MESH,
        )

    def near_copy(d):
        return pltpu.make_async_remote_copy(
            src_ref=mid,
            dst_ref=got2.at[d],
            send_sem=s2sem.at[d],
            recv_sem=r2sem.at[d],
            device_id=(near_peers[d - 1], q),
            device_id_type=MESH,
        )

    for d in range(1, far):
        far_copy(d).start()
    value = gsum[pl.ds(pl.multiple_of(z * near, near), near), :]
    for d in range(1, far):
        far_copy(d).wait()
        value += got1[d]
    mid[...] = value
    for d in range(1, near):
        near_copy(d).start()
    for d in range(1, near):
        near_copy(d).wait()
        value += got2[d]
    got2[0] = value
    row = got2[0, pl.ds(yc, 1), :]
    out_corr[...] = row[:, 0:width]
    out_proj[...] = row[:, width : 2 * width]


def per_device(
    start_block, stiffness, cell_scale, node_weight, cell_count, conn, send_rows, filter_bounds
):
    width, owned = start_block.shape
    ghost = send_rows.shape[1]
    npc, cells = conn.shape
    parts = lax.axis_size("cells")
    cols = lax.axis_size("cols")
    inner = parts // 8
    slots = -(-npc // LANES) * LANES
    half = (owned + 2 * ghost) // ghost * width
    steps = DEGREE + 2
    cfg = (width, owned, ghost, npc, cells, parts, cols, inner)
    far = parts // inner
    vmem = pl.BlockSpec(memory_space=pltpu.VMEM)
    smem = pl.BlockSpec(memory_space=pltpu.SMEM)
    dma = pltpu.SemaphoreType.DMA
    rows = parts * width // parts * cols // parts
    return pl.pallas_call(
        functools.partial(kernel, cfg),
        out_shape=(
            jax.ShapeDtypeStruct((width, owned), F32),
            jax.ShapeDtypeStruct((rows, width), F32),
            jax.ShapeDtypeStruct((rows, width), F32),
        ),
        in_specs=[vmem, vmem, vmem, vmem, smem, vmem, vmem, smem],
        out_specs=(vmem, vmem, vmem),
        scratch_shapes=[
            pltpu.VMEM((slots, slots), F32),
            pltpu.VMEM((slots, 2 * slots), BF16),
            pltpu.VMEM((slots, LANES), I32),
            pltpu.VMEM((slots, LANES), I32),
            pltpu.VMEM((LANES, slots), I32),
            pltpu.VMEM((16, LANES), I32),
            pltpu.VMEM((LANES, LANES), F32),
            pltpu.VMEM((LANES, slots), F32),
            pltpu.VMEM((LANES, slots), F32),
            pltpu.VMEM((cells * slots, ghost), BF16),
            pltpu.VMEM((cells * half, slots), BF16),
            pltpu.VMEM((half, ghost), F32),
            pltpu.VMEM((half, ghost), F32),
            pltpu.VMEM((half, ghost), F32),
            pltpu.VMEM((CHUNK * width, slots), F32),
            pltpu.VMEM((CHUNK * width, slots), F32),
            pltpu.VMEM((2 * half, CHUNK * slots), BF16),
            pltpu.VMEM((2 * half, ghost), F32),
            pltpu.VMEM((steps, half, ghost), F32),
            pltpu.VMEM((steps, 2 * width, ghost), F32),
            pltpu.VMEM((steps, 2 * width, ghost), F32),
            pltpu.VMEM((cols, half - 2 * width, ghost), F32),
            pltpu.VMEM((width * cols, LANES), F32),
            pltpu.VMEM((far, inner, LANES), F32),
            pltpu.VMEM((inner, LANES), F32),
            pltpu.VMEM((inner, inner, LANES), F32),
            dma((2, steps)),
            dma((2, steps)),
            dma((cols,)),
            dma((cols,)),
            dma((far,)),
            dma((far,)),
            dma((inner,)),
            dma((inner,)),
        ],
        compiler_params=pltpu.CompilerParams(
            collective_id=0, has_side_effects=True, vmem_limit_bytes=52 * 1024 * 1024
        ),
    )(
        start_block,
        stiffness,
        cell_scale.reshape(1, cells),
        node_weight,
        cell_count.reshape(1, 1),
        conn,
        send_rows,
        filter_bounds.reshape(1, 2),
    )


def solution(mesh):
    placed = (
        P("cols", "cells"),
        P(),
        P("cells"),
        P(None, "cells"),
        P("cells"),
        P(None, "cells"),
        P("cells", None),
        P(),
    )
    return jax.shard_map(
        per_device,
        mesh=mesh,
        in_specs=placed,
        out_specs=(P("cols", "cells"), P("cells", "cols"), P("cells", "cols")),
        check_vma=False,
    )
```

```python
import functools

import jax
import jax.numpy as jnp
from jax import lax
from jax.experimental import pallas as pl
from jax.experimental.pallas import tpu as pltpu
from jax.sharding import PartitionSpec as P

DEGREE = 4
MULT = 10
LANES = 128
CHUNK = 8
BF16 = jnp.bfloat16
F32 = jnp.float32
I32 = jnp.int32
MESH = pl.DeviceIdType.MESH


def iota(shape, dim):
    return lax.broadcasted_iota(I32, shape, dim)


def split(x):
    high = x.astype(BF16)
    return high, (x - high.astype(F32)).astype(BF16)


def dot(a, b):
    return jnp.dot(a, b, preferred_element_type=F32)


def dot_nt(a, b):
    return lax.dot_general(a, b, (((1,), (1,)), ((), ())), preferred_element_type=F32)


def pick(x, index):
    return jnp.take_along_axis(x, index, axis=1, mode="promise_in_bounds")


def mark(condition):
    return jnp.where(condition, 1.0, 0.0).astype(F32)


def kernel(
    cfg,
    start,
    stiff,
    scale,
    weight,
    count,
    conn,
    send,
    bounds,
    out_filtered,
    out_corr,
    out_proj,
    kpad,
    kk,
    newr,
    tab,
    rows_nm,
    wt,
    sc,
    onehot,
    masks,
    vcur,
    vprev,
    xall,
    xa,
    xb,
    aa,
    ab,
    acc,
    part,
    from_left,
    from_right,
    gath,
    gsum,
    got1,
    mid,
    got2,
    ssem,
    rsem,
    gssem,
    grsem,
    s1sem,
    r1sem,
    s2sem,
    r2sem,
):
    width, owned, ghost, npc, cells, parts, cols, inner = cfg
    slots = newr.shape[1]
    groups = (owned + 2 * ghost) // ghost
    half = groups * width
    tiles = 2 * groups
    near = inner
    far = parts // inner
    pair = 2 * width
    chunks = cells // CHUNK
    span = CHUNK * slots

    p = lax.axis_index("cells")
    q = lax.axis_index("cols")
    left = lax.rem(p + parts - 1, parts)
    right = lax.rem(p + 1, parts)
    z = lax.div(p, near)
    yc = lax.rem(p, near)

    far_peers = [lax.rem(z + d, far) * near + yc for d in range(1, far)]
    near_peers = [z * near + lax.rem(yc + d, near) for d in range(1, near)]
    col_peers = [lax.rem(q + d, cols) for d in range(1, cols)]

    barrier = pltpu.get_barrier_semaphore()
    targets = [(left, q), (right, q)]
    targets += [(p, other) for other in col_peers]
    targets += [(other, q) for other in far_peers]
    targets += [(other, q) for other in near_peers]
    for target in targets:
        pl.semaphore_signal(barrier, inc=1, device_id=target, device_id_type=MESH)

    lane = iota((1, LANES), 1)
    per_side = owned // 2 // LANES
    rows_nm[...] = jnp.zeros_like(rows_nm)
    places = []
    for side in range(2):
        column = jnp.broadcast_to(send[side : side + 1, :].astype(F32), (LANES, ghost)).T
        order = (iota((ghost, LANES), 0) + 1).astype(F32)
        for t in range(per_side):
            tile = side * per_side + t
            here = (iota((ghost, LANES), 1) + tile * LANES).astype(F32)
            place = jnp.sum(jnp.where(column == here, order, 0.0), axis=0, keepdims=True)
            places.append(place)
            rows_nm[tile : tile + 1, :] = mark(place == 0.0)
    free = rows_nm[...].astype(BF16)
    before = mark(iota((LANES, LANES), 0) < iota((LANES, LANES), 1)).astype(BF16)
    above = mark(iota((LANES, LANES), 0) > iota((LANES, LANES), 1)).astype(BF16)
    ones = jnp.ones((LANES, LANES), BF16)
    rank = dot(free, before) + dot(above, dot(free, ones).astype(BF16))
    base = (ghost, owned)
    for tile in range(2 * per_side):
        place = places[tile]
        shared = place + float(base[tile // per_side] - 1)
        inside = rank[tile : tile + 1, :] + float(2 * ghost)
        tab[tile : tile + 1, :] = jnp.where(place > 0.0, shared, inside).astype(I32)
    for t in range(ghost // LANES):
        a = 2 * per_side + t
        b = a + ghost // LANES
        tab[a : a + 1, :] = lane + t * LANES
        tab[b : b + 1, :] = lane + (owned + ghost + t * LANES)

    tab_cols = jnp.concatenate([tab[...], jnp.zeros((LANES - tiles, LANES), I32)], axis=0).astype(F32).T.astype(I32)
    total = jnp.zeros((2 * half, ghost), F32)
    for t in range(owned // LANES):
        high, low = split(start[:, t * LANES : (t + 1) * LANES])
        group = jnp.broadcast_to(tab[t : t + 1, :] >> 8, (half, LANES))
        member = mark(group == iota((half, LANES), 0) // width).astype(BF16)
        left_side = jnp.concatenate(
            [jnp.concatenate([high] * groups, axis=0) * member, jnp.concatenate([low] * groups, axis=0) * member], axis=0
        )
        column = jnp.broadcast_to(tab_cols[:, t : t + 1] & (ghost - 1), (LANES, ghost))
        total += dot(left_side, mark(column == iota((LANES, ghost), 1)).astype(BF16))
    part[0] = total[0:half] + total[half:]

    def to_left(step):
        return pltpu.make_async_remote_copy(
            src_ref=part.at[step, pl.ds(0, pair)],
            dst_ref=from_right.at[step],
            send_sem=ssem.at[0, step],
            recv_sem=rsem.at[0, step],
            device_id=(left, q),
            device_id_type=MESH,
        )

    def to_right(step):
        return pltpu.make_async_remote_copy(
            src_ref=part.at[step, pl.ds(half - pair, pair)],
            dst_ref=from_left.at[step],
            send_sem=ssem.at[1, step],
            recv_sem=rsem.at[1, step],
            device_id=(right, q),
            device_id_type=MESH,
        )

    def begin(step):
        to_left(step).start()
        to_right(step).start()

    has_left = jnp.where(p > 0, 1.0, 0.0).astype(F32)
    has_right = jnp.where(p < parts - 1, 1.0, 0.0).astype(F32)
    center = bounds[0, 0]
    inverse = 1.0 / jnp.full((1, ghost), bounds[0, 1], F32)

    def advance(step, rows, applied):
        current = vcur[rows, :]
        doubled = jnp.where(step > 1, 2.0, 1.0).astype(F32)
        first = jnp.where(step > 0, 0.0, 1.0).astype(F32)
        factor = inverse * (doubled * (1.0 - first)) + first
        following = (applied - (center * (1.0 - first)) * current) * factor - vprev[rows, :]
        vprev[rows, :] = current
        vcur[rows, :] = following

    def finish(step):
        to_left(step).wait()
        to_right(step).wait()
        a = (part[step, 0:width, :] + from_left[step, 0:width, :]) * has_left
        b = part[step, width:pair, :] + from_left[step, width:pair, :] * has_left
        advance(step, slice(0, pair), jnp.concatenate([a, b], axis=0))
        c = part[step, half - pair : half - width, :] + from_right[step, 0:width, :] * has_right
        d = (part[step, half - width : half, :] + from_right[step, width:pair, :]) * has_right
        advance(step, slice(half - pair, half), jnp.concatenate([c, d], axis=0))

    pl.semaphore_wait(barrier, len(targets))
    begin(0)
    vcur[...] = jnp.zeros_like(vcur)
    vprev[...] = jnp.zeros_like(vprev)
    advance(0, slice(pair, half - pair), part[0, pair : half - pair, :])

    kpad[...] = jnp.zeros_like(kpad)
    kpad[0:npc, 0:npc] = stiff[...]
    k_high, k_low = split(kpad[...].T)
    kk[0:slots, :] = k_high
    kk[slots : 2 * slots, :] = k_high
    kk[2 * slots :, :] = k_low

    newr[...] = jnp.zeros_like(newr)
    newr[:, 0:npc] = conn[...]
    for l in range(slots // LANES):
        index = newr[:, l * LANES : (l + 1) * LANES]
        low = index & (LANES - 1)
        tile = index >> 7
        value = None
        for t in range(tiles):
            got = pick(jnp.broadcast_to(tab[t : t + 1, :], (cells, LANES)), low)
            value = got if value is None else jnp.where(tile == t, got, value)
        newr[:, l * LANES : (l + 1) * LANES] = value

    live = mark(iota((cells, slots), 0) < count[0, 0]) * (1.0 / MULT)
    wt[...] = jnp.zeros_like(wt)
    wt[:, 0:npc] = weight[...]
    wt[...] = wt[...] * live
    scale_row = jnp.concatenate([scale[...], jnp.zeros((1, LANES - cells), F32)], axis=1)
    scale_col = jnp.broadcast_to(scale_row, (LANES, LANES)).T
    sc[...] = jnp.concatenate([scale_col[0:cells]] * (slots // LANES), axis=1) * live

    @pl.loop(0, cells)
    def _(c):
        index = newr[pl.ds(c, 1), :]
        place = (index & (ghost - 1)).astype(F32).astype(BF16)
        hit = jnp.broadcast_to(place, (ghost, slots)) == iota((ghost, slots), 0).astype(F32).astype(BF16)
        onehot[:, pl.ds(pl.multiple_of(c * slots, LANES), slots)] = jnp.where(
            hit, jnp.ones((), BF16), jnp.zeros((), BF16)
        )
        group = (index >> 8).astype(F32).astype(BF16)
        member = jnp.broadcast_to(group, (half, slots)) == (iota((half, slots), 0) // width).astype(F32).astype(BF16)
        masks[pl.ds(pl.multiple_of(c * half, half), half), :] = jnp.where(
            member, jnp.ones((), BF16), jnp.zeros((), BF16)
        )

    inner_tiles = range(4, tiles - 4)
    outer_tiles = list(range(4)) + list(range(tiles - 4, tiles))

    def collect(cell, group, which, value):
        index = jnp.broadcast_to(newr[pl.ds(cell, 1), :][:, group * LANES : (group + 1) * LANES], (width, LANES))
        low = index & (LANES - 1)
        tile = index >> 7
        for t in which:
            source = vcur[(t // 2) * width : (t // 2 + 1) * width, (t % 2) * LANES : (t % 2 + 1) * LANES]
            value = jnp.where(tile == t, pick(source, low), value)
        return value

    def rows_of(cell):
        return pl.ds(pl.multiple_of(cell * width, width), width)

    def gather_inner(chunk):
        for c in range(CHUNK):
            cell = chunk * CHUNK + c
            for l in range(slots // LANES):
                value = collect(cell, l, inner_tiles, jnp.zeros((width, LANES), F32))
                xall[rows_of(cell), l * LANES : (l + 1) * LANES] = value

    def gather_outer(chunk, x):
        for c in range(CHUNK):
            cell = chunk * CHUNK + c
            for l in range(slots // LANES):
                cut = slice(l * LANES, (l + 1) * LANES)
                x[c * width : (c + 1) * width, cut] = collect(cell, l, outer_tiles, xall[rows_of(cell), cut])

    def spread(chunk, x, a):
        local = x[...]
        high, low = split(local)
        wide = dot(jnp.concatenate([high, low, high], axis=1), kk[...])
        for c in range(CHUNK):
            cell = chunk * CHUNK + c
            rows = slice(c * width, (c + 1) * width)
            term = wide[rows] * sc[pl.ds(cell, 1), :] + local[rows] * wt[pl.ds(cell, 1), :]
            high, low = split(term)
            for g in range(groups):
                member = masks[pl.ds(pl.multiple_of(cell * half + g * width, width), width), :]
                a[g * width : (g + 1) * width, c * slots : (c + 1) * slots] = high * member
                a[half + g * width : half + (g + 1) * width, c * slots : (c + 1) * slots] = low * member

    def scatter(chunk, a):
        acc[...] += dot_nt(a[...], onehot[:, pl.ds(pl.multiple_of(chunk * span, LANES), span)])

    def gather_copy(d):
        return pltpu.make_async_remote_copy(
            src_ref=vcur,
            dst_ref=gath.at[d - 1],
            send_sem=gssem.at[d],
            recv_sem=grsem.at[d],
            device_id=(p, col_peers[d - 1]),
            device_id_type=MESH,
        )

    last = DEGREE + 1

    @pl.loop(1, last + 1)
    def _(step):
        @pl.loop(0, chunks)
        def _(i):
            gather_inner(i)

        finish(step - 1)

        @pl.when(step == last)
        def _():
            for d in range(1, cols):
                gather_copy(d).start()

        acc[...] = jnp.zeros_like(acc)
        gather_outer(0, xa)
        gather_outer(1, xb)
        spread(0, xa, aa)

        @pl.loop(0, chunks // 2 - 1)
        def _(i):
            n = 2 * i
            spread(n + 1, xb, ab)
            gather_outer(n + 2, xa)
            scatter(n, aa)
            spread(n + 2, xa, aa)
            gather_outer(n + 3, xb)
            scatter(n + 1, ab)

        spread(chunks - 1, xb, ab)
        scatter(chunks - 2, aa)
        scatter(chunks - 1, ab)
        part[step] = acc[0:half, :] + acc[half:, :]

        @pl.when(step < last)
        def _():
            begin(step)
            advance(step, slice(pair, half - pair), part[step, pair : half - pair, :])

    for d in range(1, cols):
        gather_copy(d).wait()

    gram = jnp.zeros((cols * width, 2 * width), F32)
    for g in range(groups):
        rows = slice(g * width, (g + 1) * width)
        mine = part[last, rows, :]
        if 0 < g < groups - 1:
            mine = jnp.concatenate([vcur[rows, :], mine], axis=0)
        else:
            mine = jnp.concatenate([jnp.zeros_like(mine), mine], axis=0)
        all_rows = jnp.concatenate([vcur[rows, :]] + [gath[d, rows, :] for d in range(cols - 1)], axis=0)
        mine_high, mine_low = split(mine)
        all_high, all_low = split(all_rows)
        gram += dot_nt(all_high, mine_high) + dot_nt(all_high, mine_low) + dot_nt(all_low, mine_high)
    gram = gram * (1.0 / (parts * owned))
    gsum[...] = jnp.zeros_like(gsum)
    for d in range(cols):
        group = lax.rem(q + cols - d, cols)
        gsum[pl.ds(pl.multiple_of(group * width, width), width), 0 : 2 * width] = gram[d * width : (d + 1) * width]

    def far_copy(d):
        block = lax.rem(z + d, far) * near
        return pltpu.make_async_remote_copy(
            src_ref=gsum.at[pl.ds(pl.multiple_of(block, near), near)],
            dst_ref=got1.at[d],
            send_sem=s1sem.at[d],
            recv_sem=r1sem.at[d],
            device_id=(far_peers[d - 1], q),
            device_id_type=MESH,
        )

    def near_copy(d):
        return pltpu.make_async_remote_copy(
            src_ref=mid,
            dst_ref=got2.at[d],
            send_sem=s2sem.at[d],
            recv_sem=r2sem.at[d],
            device_id=(near_peers[d - 1], q),
            device_id_type=MESH,
        )

    for d in range(1, far):
        far_copy(d).start()

    for t in range(owned // LANES):
        index = jnp.broadcast_to(tab[t : t + 1, :], (width, LANES))
        low = index & (LANES - 1)
        tile = index >> 7
        value = None
        for s in range(2, tiles - 2):
            source = vcur[(s // 2) * width : (s // 2 + 1) * width, (s % 2) * LANES : (s % 2 + 1) * LANES]
            got = pick(source, low)
            value = got if value is None else jnp.where(tile == s, got, value)
        out_filtered[:, t * LANES : (t + 1) * LANES] = value

    value = gsum[pl.ds(pl.multiple_of(z * near, near), near), :]
    for d in range(1, far):
        far_copy(d).wait()
        value += got1[d]
    mid[...] = value
    for d in range(1, near):
        near_copy(d).start()
    for d in range(1, near):
        near_copy(d).wait()
        value += got2[d]
    got2[0] = value
    row = got2[0, pl.ds(yc, 1), :]
    out_corr[...] = row[:, 0:width]
    out_proj[...] = row[:, width : 2 * width]


def per_device(
    start_block, stiffness, cell_scale, node_weight, cell_count, conn, send_rows, filter_bounds
):
    width, owned = start_block.shape
    ghost = send_rows.shape[1]
    npc, cells = conn.shape
    parts = lax.axis_size("cells")
    cols = lax.axis_size("cols")
    inner = parts // 8
    far = parts // inner
    slots = -(-npc // LANES) * LANES
    half = (owned + 2 * ghost) // ghost * width
    steps = DEGREE + 2
    cfg = (width, owned, ghost, npc, cells, parts, cols, inner)
    vmem = pl.BlockSpec(memory_space=pltpu.VMEM)
    smem = pl.BlockSpec(memory_space=pltpu.SMEM)
    dma = pltpu.SemaphoreType.DMA
    rows = cols * width // parts
    return pl.pallas_call(
        functools.partial(kernel, cfg),
        out_shape=(
            jax.ShapeDtypeStruct((width, owned), F32),
            jax.ShapeDtypeStruct((rows, width), F32),
            jax.ShapeDtypeStruct((rows, width), F32),
        ),
        in_specs=[vmem, vmem, vmem, vmem, smem, vmem, vmem, smem],
        out_specs=(vmem, vmem, vmem),
        scratch_shapes=[
            pltpu.VMEM((slots, slots), F32),
            pltpu.VMEM((3 * slots, slots), BF16),
            pltpu.VMEM((cells, slots), I32),
            pltpu.VMEM((16, LANES), I32),
            pltpu.VMEM((LANES, LANES), F32),
            pltpu.VMEM((cells, slots), F32),
            pltpu.VMEM((cells, slots), F32),
            pltpu.VMEM((ghost, cells * slots), BF16),
            pltpu.VMEM((cells * half, slots), BF16),
            pltpu.VMEM((half, ghost), F32),
            pltpu.VMEM((half, ghost), F32),
            pltpu.VMEM((cells * width, slots), F32),
            pltpu.VMEM((CHUNK * width, slots), F32),
            pltpu.VMEM((CHUNK * width, slots), F32),
            pltpu.VMEM((2 * half, CHUNK * slots), BF16),
            pltpu.VMEM((2 * half, CHUNK * slots), BF16),
            pltpu.VMEM((2 * half, ghost), F32),
            pltpu.VMEM((steps, half, ghost), F32),
            pltpu.VMEM((steps, 2 * width, ghost), F32),
            pltpu.VMEM((steps, 2 * width, ghost), F32),
            pltpu.VMEM((cols - 1, half, ghost), F32),
            pltpu.VMEM((width * cols, LANES), F32),
            pltpu.VMEM((far, inner, LANES), F32),
            pltpu.VMEM((inner, LANES), F32),
            pltpu.VMEM((inner, inner, LANES), F32),
            dma((2, steps)),
            dma((2, steps)),
            dma((cols,)),
            dma((cols,)),
            dma((far,)),
            dma((far,)),
            dma((inner,)),
            dma((inner,)),
        ],
        compiler_params=pltpu.CompilerParams(
            collective_id=0, has_side_effects=True, vmem_limit_bytes=52 * 1024 * 1024
        ),
    )(
        start_block,
        stiffness,
        cell_scale.reshape(1, cells),
        node_weight.T,
        cell_count.reshape(1, 1),
        conn.T,
        send_rows,
        filter_bounds.reshape(1, 2),
    )


def solution(mesh):
    placed = (
        P("cols", "cells"),
        P(),
        P("cells"),
        P(None, "cells"),
        P("cells"),
        P(None, "cells"),
        P("cells", None),
        P(),
    )
    return jax.shard_map(
        per_device,
        mesh=mesh,
        in_specs=placed,
        out_specs=(P("cols", "cells"), P("cells", "cols"), P("cells", "cols")),
        check_vma=False,
    )
```

```python
import functools

import jax
import jax.numpy as jnp
from jax import lax
from jax.experimental import pallas as pl
from jax.experimental.pallas import tpu as pltpu
from jax.sharding import PartitionSpec as P

DEGREE = 4
MULT = 10
LANES = 128
CHUNK = 8
BF16 = jnp.bfloat16
F32 = jnp.float32
I32 = jnp.int32
MESH = pl.DeviceIdType.MESH


def iota(shape, dim):
    return lax.broadcasted_iota(I32, shape, dim)


def split(x):
    high = x.astype(BF16)
    return high, (x - high.astype(F32)).astype(BF16)


def dot(a, b):
    return jnp.dot(a, b, preferred_element_type=F32)


def dot_nt(a, b):
    return lax.dot_general(a, b, (((1,), (1,)), ((), ())), preferred_element_type=F32)


def pick(x, index):
    return jnp.take_along_axis(x, index, axis=1, mode="promise_in_bounds")


def mark(condition):
    return jnp.where(condition, 1.0, 0.0).astype(F32)


def kernel(
    cfg,
    start_hbm,
    stiff_hbm,
    scale_hbm,
    weight_hbm,
    count,
    conn_hbm,
    send_hbm,
    bounds,
    out_filtered,
    out_corr,
    out_proj,
    start,
    stiff,
    scale,
    weight,
    conn,
    send,
    insem,
    kpad,
    kk,
    newr,
    tab,
    rows_nm,
    wt,
    sc,
    onehot,
    masks,
    vcur,
    vprev,
    xall,
    xa,
    xb,
    aa,
    ab,
    acc,
    part,
    from_left,
    from_right,
    gath,
    gsum,
    rowbuf,
    ssem,
    rsem,
    gssem,
    grsem,
    s1sem,
    r1sem,
):
    width, owned, ghost, npc, cells, parts, cols = cfg
    slots = newr.shape[1]
    groups = (owned + 2 * ghost) // ghost
    half = groups * width
    tiles = 2 * groups
    pair = 2 * width
    chunks = cells // CHUNK
    span = CHUNK * slots

    p = lax.axis_index("cells")
    q = lax.axis_index("cols")
    left = lax.rem(p + parts - 1, parts)
    right = lax.rem(p + 1, parts)
    col_peers = [lax.rem(q + d, cols) for d in range(1, cols)]

    loads = [
        pltpu.make_async_copy(source, target, insem.at[i])
        for i, (source, target) in enumerate(
            [
                (send_hbm, send),
                (conn_hbm, conn),
                (start_hbm, start),
                (scale_hbm, scale),
                (weight_hbm, weight),
                (stiff_hbm, stiff),
            ]
        )
    ]
    for load in loads:
        load.start()

    barrier = pltpu.get_barrier_semaphore()
    for other in col_peers:
        pl.semaphore_signal(barrier, inc=1, device_id=(p, other), device_id_type=MESH)

    @pl.loop(1, parts)
    def _(d):
        pl.semaphore_signal(barrier, inc=1, device_id=(lax.rem(p + d, parts), q), device_id_type=MESH)

    loads[0].wait()
    lane = iota((1, LANES), 1)
    per_side = owned // 2 // LANES
    rows_nm[...] = jnp.zeros_like(rows_nm)
    places = []
    for side in range(2):
        column = jnp.broadcast_to(send[side : side + 1, :].astype(F32), (LANES, ghost)).T
        order = (iota((ghost, LANES), 0) + 1).astype(F32)
        for t in range(per_side):
            tile = side * per_side + t
            here = (iota((ghost, LANES), 1) + tile * LANES).astype(F32)
            place = jnp.sum(jnp.where(column == here, order, 0.0), axis=0, keepdims=True)
            places.append(place)
            rows_nm[tile : tile + 1, :] = mark(place == 0.0)
    free = rows_nm[...].astype(BF16)
    before = mark(iota((LANES, LANES), 0) < iota((LANES, LANES), 1)).astype(BF16)
    above = mark(iota((LANES, LANES), 0) > iota((LANES, LANES), 1)).astype(BF16)
    ones = jnp.ones((LANES, LANES), BF16)
    rank = dot(free, before) + dot(above, dot(free, ones).astype(BF16))
    base = (ghost, owned)
    for tile in range(2 * per_side):
        place = places[tile]
        shared = place + float(base[tile // per_side] - 1)
        inside = rank[tile : tile + 1, :] + float(2 * ghost)
        tab[tile : tile + 1, :] = jnp.where(place > 0.0, shared, inside).astype(I32)
    for t in range(ghost // LANES):
        a = 2 * per_side + t
        b = a + ghost // LANES
        tab[a : a + 1, :] = lane + t * LANES
        tab[b : b + 1, :] = lane + (owned + ghost + t * LANES)

    tab_cols = jnp.concatenate([tab[...], jnp.zeros((LANES - tiles, LANES), I32)], axis=0).astype(F32).T.astype(I32)
    total = jnp.zeros((2 * half, ghost), F32)
    loads[2].wait()
    for t in range(owned // LANES):
        high, low = split(start[:, t * LANES : (t + 1) * LANES])
        group = jnp.broadcast_to(tab[t : t + 1, :] >> 8, (half, LANES))
        member = mark(group == iota((half, LANES), 0) // width).astype(BF16)
        left_side = jnp.concatenate(
            [jnp.concatenate([high] * groups, axis=0) * member, jnp.concatenate([low] * groups, axis=0) * member], axis=0
        )
        column = jnp.broadcast_to(tab_cols[:, t : t + 1] & (ghost - 1), (LANES, ghost))
        total += dot(left_side, mark(column == iota((LANES, ghost), 1)).astype(BF16))
    part[0] = total[0:half] + total[half:]

    def to_left(step):
        return pltpu.make_async_remote_copy(
            src_ref=part.at[step, pl.ds(0, pair)],
            dst_ref=from_right.at[step],
            send_sem=ssem.at[0, step],
            recv_sem=rsem.at[0, step],
            device_id=(left, q),
            device_id_type=MESH,
        )

    def to_right(step):
        return pltpu.make_async_remote_copy(
            src_ref=part.at[step, pl.ds(half - pair, pair)],
            dst_ref=from_left.at[step],
            send_sem=ssem.at[1, step],
            recv_sem=rsem.at[1, step],
            device_id=(right, q),
            device_id_type=MESH,
        )

    def begin(step):
        to_left(step).start()
        to_right(step).start()

    has_left = jnp.where(p > 0, 1.0, 0.0).astype(F32)
    has_right = jnp.where(p < parts - 1, 1.0, 0.0).astype(F32)
    center = bounds[0, 0]
    inverse = 1.0 / jnp.full((1, ghost), bounds[0, 1], F32)

    def advance(step, rows, applied):
        current = vcur[rows, :]
        doubled = jnp.where(step > 1, 2.0, 1.0).astype(F32)
        first = jnp.where(step > 0, 0.0, 1.0).astype(F32)
        factor = inverse * (doubled * (1.0 - first)) + first
        following = (applied - (center * (1.0 - first)) * current) * factor - vprev[rows, :]
        vprev[rows, :] = current
        vcur[rows, :] = following

    def finish(step):
        to_left(step).wait()
        to_right(step).wait()
        a = (part[step, 0:width, :] + from_left[step, 0:width, :]) * has_left
        b = part[step, width:pair, :] + from_left[step, width:pair, :] * has_left
        advance(step, slice(0, pair), jnp.concatenate([a, b], axis=0))
        c = part[step, half - pair : half - width, :] + from_right[step, 0:width, :] * has_right
        d = (part[step, half - width : half, :] + from_right[step, width:pair, :]) * has_right
        advance(step, slice(half - pair, half), jnp.concatenate([c, d], axis=0))

    vcur[...] = jnp.zeros_like(vcur)
    vprev[...] = jnp.zeros_like(vprev)
    advance(0, slice(pair, half - pair), part[0, pair : half - pair, :])

    loads[5].wait()
    kpad[...] = jnp.zeros_like(kpad)
    kpad[0:npc, 0:npc] = stiff[...]
    k_high, k_low = split(kpad[...].T)
    kk[0:slots, :] = k_high
    kk[slots : 2 * slots, :] = k_high
    kk[2 * slots :, :] = k_low

    loads[1].wait()
    newr[...] = jnp.zeros_like(newr)
    newr[:, 0:npc] = conn[...]
    for l in range(slots // LANES):
        index = newr[:, l * LANES : (l + 1) * LANES]
        low = index & (LANES - 1)
        tile = index >> 7
        value = None
        for t in range(tiles):
            got = pick(jnp.broadcast_to(tab[t : t + 1, :], (cells, LANES)), low)
            value = got if value is None else jnp.where(tile == t, got, value)
        newr[:, l * LANES : (l + 1) * LANES] = value

    live = mark(iota((cells, slots), 0) < count[0, 0]) * (1.0 / MULT)
    loads[3].wait()
    loads[4].wait()
    wt[...] = jnp.zeros_like(wt)
    wt[:, 0:npc] = weight[...]
    wt[...] = wt[...] * live
    scale_row = jnp.concatenate([scale[...], jnp.zeros((1, LANES - cells), F32)], axis=1)
    scale_col = jnp.broadcast_to(scale_row, (LANES, LANES)).T
    sc[...] = jnp.concatenate([scale_col[0:cells]] * (slots // LANES), axis=1) * live

    @pl.loop(0, cells)
    def _(c):
        index = newr[pl.ds(c, 1), :]
        place = (index & (ghost - 1)).astype(F32).astype(BF16)
        hit = jnp.broadcast_to(place, (ghost, slots)) == iota((ghost, slots), 0).astype(F32).astype(BF16)
        onehot[:, pl.ds(pl.multiple_of(c * slots, LANES), slots)] = jnp.where(
            hit, jnp.ones((), BF16), jnp.zeros((), BF16)
        )
        group = (index >> 8).astype(F32).astype(BF16)
        member = jnp.broadcast_to(group, (half, slots)) == (iota((half, slots), 0) // width).astype(F32).astype(BF16)
        masks[pl.ds(pl.multiple_of(c * half, half), half), :] = jnp.where(
            member, jnp.ones((), BF16), jnp.zeros((), BF16)
        )

    pl.semaphore_wait(barrier, parts + cols - 2)
    begin(0)

    inner_tiles = range(4, tiles - 4)
    outer_tiles = list(range(4)) + list(range(tiles - 4, tiles))

    def collect(cell, group, which, value):
        index = jnp.broadcast_to(newr[pl.ds(cell, 1), :][:, group * LANES : (group + 1) * LANES], (width, LANES))
        low = index & (LANES - 1)
        tile = index >> 7
        for t in which:
            source = vcur[(t // 2) * width : (t // 2 + 1) * width, (t % 2) * LANES : (t % 2 + 1) * LANES]
            value = jnp.where(tile == t, pick(source, low), value)
        return value

    def rows_of(cell):
        return pl.ds(pl.multiple_of(cell * width, width), width)

    def gather_inner(chunk):
        for c in range(CHUNK):
            cell = chunk * CHUNK + c
            for l in range(slots // LANES):
                value = collect(cell, l, inner_tiles, jnp.zeros((width, LANES), F32))
                xall[rows_of(cell), l * LANES : (l + 1) * LANES] = value

    def gather_outer(chunk, x):
        for c in range(CHUNK):
            cell = chunk * CHUNK + c
            for l in range(slots // LANES):
                cut = slice(l * LANES, (l + 1) * LANES)
                x[c * width : (c + 1) * width, cut] = collect(cell, l, outer_tiles, xall[rows_of(cell), cut])

    def spread(chunk, x, a):
        local = x[...]
        high, low = split(local)
        wide = dot(jnp.concatenate([high, low, high], axis=1), kk[...])
        for c in range(CHUNK):
            cell = chunk * CHUNK + c
            rows = slice(c * width, (c + 1) * width)
            term = wide[rows] * sc[pl.ds(cell, 1), :] + local[rows] * wt[pl.ds(cell, 1), :]
            high, low = split(term)
            for g in range(groups):
                member = masks[pl.ds(pl.multiple_of(cell * half + g * width, width), width), :]
                a[g * width : (g + 1) * width, c * slots : (c + 1) * slots] = high * member
                a[half + g * width : half + (g + 1) * width, c * slots : (c + 1) * slots] = low * member

    def scatter(chunk, a):
        acc[...] += dot_nt(a[...], onehot[:, pl.ds(pl.multiple_of(chunk * span, LANES), span)])

    def gather_copy(d):
        return pltpu.make_async_remote_copy(
            src_ref=vcur,
            dst_ref=gath.at[d - 1],
            send_sem=gssem.at[d],
            recv_sem=grsem.at[d],
            device_id=(p, col_peers[d - 1]),
            device_id_type=MESH,
        )

    last = DEGREE + 1

    @pl.loop(1, last + 1)
    def _(step):
        @pl.loop(0, chunks)
        def _(i):
            gather_inner(i)

        finish(step - 1)

        @pl.when(step == last)
        def _():
            for d in range(1, cols):
                gather_copy(d).start()

        acc[...] = jnp.zeros_like(acc)
        gather_outer(0, xa)
        gather_outer(1, xb)
        spread(0, xa, aa)

        @pl.loop(0, chunks // 2 - 1)
        def _(i):
            n = 2 * i
            spread(n + 1, xb, ab)
            gather_outer(n + 2, xa)
            scatter(n, aa)
            spread(n + 2, xa, aa)
            gather_outer(n + 3, xb)
            scatter(n + 1, ab)

        spread(chunks - 1, xb, ab)
        scatter(chunks - 2, aa)
        scatter(chunks - 1, ab)
        part[step] = acc[0:half, :] + acc[half:, :]

        @pl.when(step < last)
        def _():
            begin(step)
            advance(step, slice(pair, half - pair), part[step, pair : half - pair, :])

    for d in range(1, cols):
        gather_copy(d).wait()

    gram = jnp.zeros((cols * width, 2 * width), F32)
    for g in range(groups):
        rows = slice(g * width, (g + 1) * width)
        mine = part[last, rows, :]
        if 0 < g < groups - 1:
            mine = jnp.concatenate([vcur[rows, :], mine], axis=0)
        else:
            mine = jnp.concatenate([jnp.zeros_like(mine), mine], axis=0)
        all_rows = jnp.concatenate([vcur[rows, :]] + [gath[d, rows, :] for d in range(cols - 1)], axis=0)
        mine_high, mine_low = split(mine)
        all_high, all_low = split(all_rows)
        gram += dot_nt(all_high, mine_high) + dot_nt(all_high, mine_low) + dot_nt(all_low, mine_high)
    gram = gram * (1.0 / (parts * owned))
    gsum[...] = jnp.zeros_like(gsum)
    for d in range(cols):
        group = lax.rem(q + cols - d, cols)
        gsum[pl.ds(pl.multiple_of(group * width, width), width), 0 : 2 * width] = gram[d * width : (d + 1) * width]

    def row_copy(d):
        return pltpu.make_async_remote_copy(
            src_ref=gsum.at[pl.ds(lax.rem(p + d, parts), 1)],
            dst_ref=rowbuf.at[d],
            send_sem=s1sem.at[d],
            recv_sem=r1sem.at[d],
            device_id=(lax.rem(p + d, parts), q),
            device_id_type=MESH,
        )

    @pl.loop(1, parts)
    def _(d):
        row_copy(d).start()

    rowbuf[0] = gsum[pl.ds(p, 1), :]

    for t in range(owned // LANES):
        index = jnp.broadcast_to(tab[t : t + 1, :], (width, LANES))
        low = index & (LANES - 1)
        tile = index >> 7
        value = None
        for s in range(2, tiles - 2):
            source = vcur[(s // 2) * width : (s // 2 + 1) * width, (s % 2) * LANES : (s % 2 + 1) * LANES]
            got = pick(source, low)
            value = got if value is None else jnp.where(tile == s, got, value)
        out_filtered[:, t * LANES : (t + 1) * LANES] = value

    @pl.loop(1, parts)
    def _(d):
        row_copy(d).wait()

    row = jnp.sum(rowbuf[...], axis=0)
    out_corr[...] = row[:, 0:width]
    out_proj[...] = row[:, width : 2 * width]


def per_device(
    start_block, stiffness, cell_scale, node_weight, cell_count, conn, send_rows, filter_bounds
):
    width, owned = start_block.shape
    ghost = send_rows.shape[1]
    npc, cells = conn.shape
    parts = lax.axis_size("cells")
    cols = lax.axis_size("cols")
    slots = -(-npc // LANES) * LANES
    half = (owned + 2 * ghost) // ghost * width
    steps = DEGREE + 2
    cfg = (width, owned, ghost, npc, cells, parts, cols)
    vmem = pl.BlockSpec(memory_space=pltpu.VMEM)
    hbm = pl.BlockSpec(memory_space=pltpu.HBM)
    smem = pl.BlockSpec(memory_space=pltpu.SMEM)
    dma = pltpu.SemaphoreType.DMA
    rows = cols * width // parts
    return pl.pallas_call(
        functools.partial(kernel, cfg),
        out_shape=(
            jax.ShapeDtypeStruct((width, owned), F32),
            jax.ShapeDtypeStruct((rows, width), F32),
            jax.ShapeDtypeStruct((rows, width), F32),
        ),
        in_specs=[hbm, hbm, hbm, hbm, smem, hbm, hbm, smem],
        out_specs=(vmem, vmem, vmem),
        scratch_shapes=[
            pltpu.VMEM((width, owned), F32),
            pltpu.VMEM((npc, npc), F32),
            pltpu.VMEM((1, cells), F32),
            pltpu.VMEM((cells, npc), F32),
            pltpu.VMEM((cells, npc), I32),
            pltpu.VMEM((2, ghost), I32),
            dma((6,)),
            pltpu.VMEM((slots, slots), F32),
            pltpu.VMEM((3 * slots, slots), BF16),
            pltpu.VMEM((cells, slots), I32),
            pltpu.VMEM((16, LANES), I32),
            pltpu.VMEM((LANES, LANES), F32),
            pltpu.VMEM((cells, slots), F32),
            pltpu.VMEM((cells, slots), F32),
            pltpu.VMEM((ghost, cells * slots), BF16),
            pltpu.VMEM((cells * half, slots), BF16),
            pltpu.VMEM((half, ghost), F32),
            pltpu.VMEM((half, ghost), F32),
            pltpu.VMEM((cells * width, slots), F32),
            pltpu.VMEM((CHUNK * width, slots), F32),
            pltpu.VMEM((CHUNK * width, slots), F32),
            pltpu.VMEM((2 * half, CHUNK * slots), BF16),
            pltpu.VMEM((2 * half, CHUNK * slots), BF16),
            pltpu.VMEM((2 * half, ghost), F32),
            pltpu.VMEM((steps, half, ghost), F32),
            pltpu.VMEM((steps, 2 * width, ghost), F32),
            pltpu.VMEM((steps, 2 * width, ghost), F32),
            pltpu.VMEM((cols - 1, half, ghost), F32),
            pltpu.VMEM((width * cols, LANES), F32),
            pltpu.VMEM((parts, 1, LANES), F32),
            dma((2, steps)),
            dma((2, steps)),
            dma((cols,)),
            dma((cols,)),
            dma((parts,)),
            dma((parts,)),
        ],
        compiler_params=pltpu.CompilerParams(
            collective_id=0, has_side_effects=True, vmem_limit_bytes=62 * 1024 * 1024
        ),
    )(
        start_block,
        stiffness,
        cell_scale.reshape(1, cells),
        node_weight.T,
        cell_count.reshape(1, 1),
        conn.T,
        send_rows,
        filter_bounds.reshape(1, 2),
    )


def solution(mesh):
    placed = (
        P("cols", "cells"),
        P(),
        P("cells"),
        P(None, "cells"),
        P("cells"),
        P(None, "cells"),
        P("cells", None),
        P(),
    )
    return jax.shard_map(
        per_device,
        mesh=mesh,
        in_specs=placed,
        out_specs=(P("cols", "cells"), P("cells", "cols"), P("cells", "cols")),
        check_vma=False,
    )
```

```python
import functools

import jax
import jax.numpy as jnp
from jax import lax
from jax.experimental import pallas as pl
from jax.experimental.pallas import tpu as pltpu
from jax.sharding import PartitionSpec as P

DEGREE = 4
MULT = 10
LANES = 128
CHUNK = 8
BF16 = jnp.bfloat16
F32 = jnp.float32
I32 = jnp.int32
MESH = pl.DeviceIdType.MESH


def iota(shape, dim):
    return lax.broadcasted_iota(I32, shape, dim)


def split(x):
    high = x.astype(BF16)
    return high, (x - high.astype(F32)).astype(BF16)


def dot(a, b):
    return jnp.dot(a, b, preferred_element_type=F32)


def dot_nt(a, b):
    return lax.dot_general(a, b, (((1,), (1,)), ((), ())), preferred_element_type=F32)


def pick(x, index):
    return jnp.take_along_axis(x, index, axis=1, mode="promise_in_bounds")


def mark(condition):
    return jnp.where(condition, 1.0, 0.0).astype(F32)


def kernel(
    cfg,
    start_hbm,
    stiff_hbm,
    scale_hbm,
    weight_hbm,
    count,
    conn_hbm,
    send_hbm,
    bounds,
    out_filtered,
    out_corr,
    out_proj,
    start,
    stiff,
    scale,
    weight,
    conn,
    send,
    insem,
    kpad,
    kk,
    newr,
    index8,
    weight8,
    scale8,
    tab,
    rows_nm,
    wt,
    sc,
    onehot,
    masks,
    vcur,
    vprev,
    xall,
    xa,
    xb,
    aa,
    ab,
    acc,
    part,
    from_left,
    from_right,
    gath,
    gsum,
    rowbuf,
    ssem,
    rsem,
    gssem,
    grsem,
    s1sem,
    r1sem,
):
    width, owned, ghost, npc, cells, parts, cols = cfg
    slots = newr.shape[1]
    groups = (owned + 2 * ghost) // ghost
    half = groups * width
    tiles = 2 * groups
    pair = 2 * width
    chunks = cells // CHUNK
    span = CHUNK * slots

    p = lax.axis_index("cells")
    q = lax.axis_index("cols")
    left = lax.rem(p + parts - 1, parts)
    right = lax.rem(p + 1, parts)
    col_peers = [lax.rem(q + d, cols) for d in range(1, cols)]

    loads = [
        pltpu.make_async_copy(source, target, insem.at[i])
        for i, (source, target) in enumerate(
            [
                (send_hbm, send),
                (conn_hbm, conn),
                (start_hbm, start),
                (scale_hbm, scale),
                (weight_hbm, weight),
                (stiff_hbm, stiff),
            ]
        )
    ]
    for load in loads:
        load.start()

    barrier = pltpu.get_barrier_semaphore()
    for other in col_peers:
        pl.semaphore_signal(barrier, inc=1, device_id=(p, other), device_id_type=MESH)

    @pl.loop(1, parts)
    def _(d):
        pl.semaphore_signal(barrier, inc=1, device_id=(lax.rem(p + d, parts), q), device_id_type=MESH)

    loads[0].wait()
    lane = iota((1, LANES), 1)
    per_side = owned // 2 // LANES
    rows_nm[...] = jnp.zeros_like(rows_nm)
    places = []
    for side in range(2):
        column = jnp.broadcast_to(send[side : side + 1, :].astype(F32), (LANES, ghost)).T
        order = (iota((ghost, LANES), 0) + 1).astype(F32)
        for t in range(per_side):
            tile = side * per_side + t
            here = (iota((ghost, LANES), 1) + tile * LANES).astype(F32)
            place = jnp.sum(jnp.where(column == here, order, 0.0), axis=0, keepdims=True)
            places.append(place)
            rows_nm[tile : tile + 1, :] = mark(place == 0.0)
    free = rows_nm[...].astype(BF16)
    before = mark(iota((LANES, LANES), 0) < iota((LANES, LANES), 1)).astype(BF16)
    above = mark(iota((LANES, LANES), 0) > iota((LANES, LANES), 1)).astype(BF16)
    ones = jnp.ones((LANES, LANES), BF16)
    rank = dot(free, before) + dot(above, dot(free, ones).astype(BF16))
    base = (ghost, owned)
    for tile in range(2 * per_side):
        place = places[tile]
        shared = place + float(base[tile // per_side] - 1)
        inside = rank[tile : tile + 1, :] + float(2 * ghost)
        tab[tile : tile + 1, :] = jnp.where(place > 0.0, shared, inside).astype(I32)
    for t in range(ghost // LANES):
        a = 2 * per_side + t
        b = a + ghost // LANES
        tab[a : a + 1, :] = lane + t * LANES
        tab[b : b + 1, :] = lane + (owned + ghost + t * LANES)

    tab_cols = jnp.concatenate([tab[...], jnp.zeros((LANES - tiles, LANES), I32)], axis=0).astype(F32).T.astype(I32)
    total = jnp.zeros((2 * half, ghost), F32)
    loads[2].wait()
    for t in range(owned // LANES):
        high, low = split(start[:, t * LANES : (t + 1) * LANES])
        group = jnp.broadcast_to(tab[t : t + 1, :] >> 8, (half, LANES))
        member = mark(group == iota((half, LANES), 0) // width).astype(BF16)
        left_side = jnp.concatenate(
            [jnp.concatenate([high] * groups, axis=0) * member, jnp.concatenate([low] * groups, axis=0) * member], axis=0
        )
        column = jnp.broadcast_to(tab_cols[:, t : t + 1] & (ghost - 1), (LANES, ghost))
        total += dot(left_side, mark(column == iota((LANES, ghost), 1)).astype(BF16))
    part[0] = total[0:half] + total[half:]

    def to_left(step):
        return pltpu.make_async_remote_copy(
            src_ref=part.at[step, pl.ds(0, pair)],
            dst_ref=from_right.at[step],
            send_sem=ssem.at[0, step],
            recv_sem=rsem.at[0, step],
            device_id=(left, q),
            device_id_type=MESH,
        )

    def to_right(step):
        return pltpu.make_async_remote_copy(
            src_ref=part.at[step, pl.ds(half - pair, pair)],
            dst_ref=from_left.at[step],
            send_sem=ssem.at[1, step],
            recv_sem=rsem.at[1, step],
            device_id=(right, q),
            device_id_type=MESH,
        )

    def begin(step):
        to_left(step).start()
        to_right(step).start()

    has_left = jnp.where(p > 0, 1.0, 0.0).astype(F32)
    has_right = jnp.where(p < parts - 1, 1.0, 0.0).astype(F32)
    center = bounds[0, 0]
    inverse = 1.0 / jnp.full((1, ghost), bounds[0, 1], F32)

    def advance(step, rows, applied):
        current = vcur[rows, :]
        doubled = jnp.where(step > 1, 2.0, 1.0).astype(F32)
        first = jnp.where(step > 0, 0.0, 1.0).astype(F32)
        factor = inverse * (doubled * (1.0 - first)) + first
        following = (applied - (center * (1.0 - first)) * current) * factor - vprev[rows, :]
        vprev[rows, :] = current
        vcur[rows, :] = following

    def finish(step):
        to_left(step).wait()
        to_right(step).wait()
        a = (part[step, 0:width, :] + from_left[step, 0:width, :]) * has_left
        b = part[step, width:pair, :] + from_left[step, width:pair, :] * has_left
        advance(step, slice(0, pair), jnp.concatenate([a, b], axis=0))
        c = part[step, half - pair : half - width, :] + from_right[step, 0:width, :] * has_right
        d = (part[step, half - width : half, :] + from_right[step, width:pair, :]) * has_right
        advance(step, slice(half - pair, half), jnp.concatenate([c, d], axis=0))

    vcur[...] = jnp.zeros_like(vcur)
    vprev[...] = jnp.zeros_like(vprev)
    advance(0, slice(pair, half - pair), part[0, pair : half - pair, :])

    loads[5].wait()
    kpad[...] = jnp.zeros_like(kpad)
    kpad[0:npc, 0:npc] = stiff[...]
    k_high, k_low = split(kpad[...].T)
    kk[0:slots, :] = k_high
    kk[slots : 2 * slots, :] = k_high
    kk[2 * slots :, :] = k_low

    loads[1].wait()
    newr[...] = jnp.zeros_like(newr)
    newr[:, 0:npc] = conn[...]
    for l in range(slots // LANES):
        index = newr[:, l * LANES : (l + 1) * LANES]
        low = index & (LANES - 1)
        tile = index >> 7
        value = None
        for t in range(tiles):
            got = pick(jnp.broadcast_to(tab[t : t + 1, :], (cells, LANES)), low)
            value = got if value is None else jnp.where(tile == t, got, value)
        newr[:, l * LANES : (l + 1) * LANES] = value

    live = mark(iota((cells, slots), 0) < count[0, 0]) * (1.0 / MULT)
    loads[3].wait()
    loads[4].wait()
    wt[...] = jnp.zeros_like(wt)
    wt[:, 0:npc] = weight[...]
    wt[...] = wt[...] * live
    scale_row = jnp.concatenate([scale[...], jnp.zeros((1, LANES - cells), F32)], axis=1)
    scale_col = jnp.broadcast_to(scale_row, (LANES, LANES)).T
    sc[...] = jnp.concatenate([scale_col[0:cells]] * (slots // LANES), axis=1) * live

    @pl.loop(0, cells)
    def _(c):
        index = newr[pl.ds(c, 1), :]
        rows = pl.ds(pl.multiple_of(c * 8, 8), 8)
        index8[rows, :] = jnp.broadcast_to(index, (8, slots))
        weight8[rows, :] = jnp.broadcast_to(wt[pl.ds(c, 1), :], (8, slots))
        scale8[rows, :] = jnp.broadcast_to(sc[pl.ds(c, 1), :], (8, slots))
        place = (index & (ghost - 1)).astype(F32).astype(BF16)
        hit = jnp.broadcast_to(place, (ghost, slots)) == iota((ghost, slots), 0).astype(F32).astype(BF16)
        onehot[:, pl.ds(pl.multiple_of(c * slots, LANES), slots)] = jnp.where(
            hit, jnp.ones((), BF16), jnp.zeros((), BF16)
        )
        group = (index >> 8).astype(F32).astype(BF16)
        member = jnp.broadcast_to(group, (half, slots)) == (iota((half, slots), 0) // width).astype(F32).astype(BF16)
        masks[pl.ds(pl.multiple_of(c * half, half), half), :] = jnp.where(
            member, jnp.ones((), BF16), jnp.zeros((), BF16)
        )

    pl.semaphore_wait(barrier, parts + cols - 2)
    begin(0)

    inner_tiles = range(4, tiles - 4)
    outer_tiles = list(range(4)) + list(range(tiles - 4, tiles))

    def twice(x):
        return jnp.concatenate([x, x], axis=0)

    def collect(cell, group, which, value):
        index = twice(index8[pl.ds(pl.multiple_of(cell * 8, 8), 8), group * LANES : (group + 1) * LANES])
        low = index & (LANES - 1)
        tile = index >> 7
        for t in which:
            source = vcur[(t // 2) * width : (t // 2 + 1) * width, (t % 2) * LANES : (t % 2 + 1) * LANES]
            value = jnp.where(tile == t, pick(source, low), value)
        return value

    def rows_of(cell):
        return pl.ds(pl.multiple_of(cell * width, width), width)

    turns = chunks // 2 - 1
    late = 3 * turns
    early = cells - late

    def gather_inner(first, number):
        for c in range(number):
            cell = first + c
            for l in range(slots // LANES):
                value = collect(cell, l, inner_tiles, jnp.zeros((width, LANES), F32))
                xall[rows_of(cell), l * LANES : (l + 1) * LANES] = value

    def gather_outer(chunk, x):
        for c in range(CHUNK):
            cell = chunk * CHUNK + c
            for l in range(slots // LANES):
                cut = slice(l * LANES, (l + 1) * LANES)
                x[c * width : (c + 1) * width, cut] = collect(cell, l, outer_tiles, xall[rows_of(cell), cut])

    def spread(chunk, x, a):
        local = x[...]
        high, low = split(local)
        wide = dot(jnp.concatenate([high, low, high], axis=1), kk[...])
        for c in range(CHUNK):
            cell = chunk * CHUNK + c
            rows = slice(c * width, (c + 1) * width)
            eight = pl.ds(pl.multiple_of(cell * 8, 8), 8)
            term = wide[rows] * twice(scale8[eight, :]) + local[rows] * twice(weight8[eight, :])
            high, low = split(term)
            for g in range(groups):
                member = masks[pl.ds(pl.multiple_of(cell * half + g * width, width), width), :]
                a[g * width : (g + 1) * width, c * slots : (c + 1) * slots] = high * member
                a[half + g * width : half + (g + 1) * width, c * slots : (c + 1) * slots] = low * member

    def scatter(chunk, a):
        acc[...] += dot_nt(a[...], onehot[:, pl.ds(pl.multiple_of(chunk * span, LANES), span)])

    def gather_copy(d):
        return pltpu.make_async_remote_copy(
            src_ref=vcur,
            dst_ref=gath.at[d - 1],
            send_sem=gssem.at[d],
            recv_sem=grsem.at[d],
            device_id=(p, col_peers[d - 1]),
            device_id_type=MESH,
        )

    last = DEGREE + 1

    @pl.loop(1, last + 1)
    def _(step):
        @pl.loop(0, early // 5)
        def _(i):
            gather_inner(i * 5, 5)

        finish(step - 1)

        @pl.when(step == last)
        def _():
            for d in range(1, cols):
                gather_copy(d).start()

        acc[...] = jnp.zeros_like(acc)
        gather_outer(0, xa)
        gather_outer(1, xb)
        spread(0, xa, aa)

        @pl.loop(0, chunks // 2 - 1)
        def _(i):
            n = 2 * i
            gather_inner(early + 3 * i, 3)
            spread(n + 1, xb, ab)
            gather_outer(n + 2, xa)
            scatter(n, aa)
            spread(n + 2, xa, aa)
            gather_outer(n + 3, xb)
            scatter(n + 1, ab)

        spread(chunks - 1, xb, ab)
        scatter(chunks - 2, aa)
        scatter(chunks - 1, ab)
        part[step] = acc[0:half, :] + acc[half:, :]

        @pl.when(step < last)
        def _():
            begin(step)
            advance(step, slice(pair, half - pair), part[step, pair : half - pair, :])

    for d in range(1, cols):
        gather_copy(d).wait()

    gram = jnp.zeros((cols * width, 2 * width), F32)
    for g in range(groups):
        rows = slice(g * width, (g + 1) * width)
        mine = part[last, rows, :]
        if 0 < g < groups - 1:
            mine = jnp.concatenate([vcur[rows, :], mine], axis=0)
        else:
            mine = jnp.concatenate([jnp.zeros_like(mine), mine], axis=0)
        all_rows = jnp.concatenate([vcur[rows, :]] + [gath[d, rows, :] for d in range(cols - 1)], axis=0)
        mine_high, mine_low = split(mine)
        all_high, all_low = split(all_rows)
        gram += dot_nt(all_high, mine_high) + dot_nt(all_high, mine_low) + dot_nt(all_low, mine_high)
    gram = gram * (1.0 / (parts * owned))
    gsum[...] = jnp.zeros_like(gsum)
    for d in range(cols):
        group = lax.rem(q + cols - d, cols)
        gsum[pl.ds(pl.multiple_of(group * width, width), width), 0 : 2 * width] = gram[d * width : (d + 1) * width]

    def row_copy(d):
        return pltpu.make_async_remote_copy(
            src_ref=gsum.at[pl.ds(lax.rem(p + d, parts), 1)],
            dst_ref=rowbuf.at[d],
            send_sem=s1sem,
            recv_sem=r1sem,
            device_id=(lax.rem(p + d, parts), q),
            device_id_type=MESH,
        )

    middle = parts // 2
    row_copy(middle).start()

    @pl.loop(1, middle)
    def _(j):
        row_copy(middle - j).start()
        row_copy(middle + j).start()

    rowbuf[0] = gsum[pl.ds(p, 1), :]

    for t in range(owned // LANES):
        index = jnp.broadcast_to(tab[t : t + 1, :], (width, LANES))
        low = index & (LANES - 1)
        tile = index >> 7
        value = None
        for s in range(2, tiles - 2):
            source = vcur[(s // 2) * width : (s // 2 + 1) * width, (s % 2) * LANES : (s % 2 + 1) * LANES]
            got = pick(source, low)
            value = got if value is None else jnp.where(tile == s, got, value)
        out_filtered[:, t * LANES : (t + 1) * LANES] = value

    every = pltpu.make_async_remote_copy(
        src_ref=rowbuf.at[pl.ds(1, parts - 1)],
        dst_ref=rowbuf.at[pl.ds(1, parts - 1)],
        send_sem=s1sem,
        recv_sem=r1sem,
        device_id=(right, q),
        device_id_type=MESH,
    )
    every.wait_send()
    every.wait_recv()
    row = jnp.sum(rowbuf[...], axis=0)
    out_corr[...] = row[:, 0:width]
    out_proj[...] = row[:, width : 2 * width]


def per_device(
    start_block, stiffness, cell_scale, node_weight, cell_count, conn, send_rows, filter_bounds
):
    width, owned = start_block.shape
    ghost = send_rows.shape[1]
    npc, cells = conn.shape
    parts = lax.axis_size("cells")
    cols = lax.axis_size("cols")
    slots = -(-npc // LANES) * LANES
    half = (owned + 2 * ghost) // ghost * width
    steps = DEGREE + 2
    cfg = (width, owned, ghost, npc, cells, parts, cols)
    vmem = pl.BlockSpec(memory_space=pltpu.VMEM)
    hbm = pl.BlockSpec(memory_space=pltpu.HBM)
    smem = pl.BlockSpec(memory_space=pltpu.SMEM)
    dma = pltpu.SemaphoreType.DMA
    rows = cols * width // parts
    return pl.pallas_call(
        functools.partial(kernel, cfg),
        out_shape=(
            jax.ShapeDtypeStruct((width, owned), F32),
            jax.ShapeDtypeStruct((rows, width), F32),
            jax.ShapeDtypeStruct((rows, width), F32),
        ),
        in_specs=[hbm, hbm, hbm, hbm, smem, hbm, hbm, smem],
        out_specs=(vmem, vmem, vmem),
        scratch_shapes=[
            pltpu.VMEM((width, owned), F32),
            pltpu.VMEM((npc, npc), F32),
            pltpu.VMEM((1, cells), F32),
            pltpu.VMEM((cells, npc), F32),
            pltpu.VMEM((cells, npc), I32),
            pltpu.VMEM((2, ghost), I32),
            dma((6,)),
            pltpu.VMEM((slots, slots), F32),
            pltpu.VMEM((3 * slots, slots), BF16),
            pltpu.VMEM((cells, slots), I32),
            pltpu.VMEM((cells * 8, slots), I32),
            pltpu.VMEM((cells * 8, slots), F32),
            pltpu.VMEM((cells * 8, slots), F32),
            pltpu.VMEM((16, LANES), I32),
            pltpu.VMEM((LANES, LANES), F32),
            pltpu.VMEM((cells, slots), F32),
            pltpu.VMEM((cells, slots), F32),
            pltpu.VMEM((ghost, cells * slots), BF16),
            pltpu.VMEM((cells * half, slots), BF16),
            pltpu.VMEM((half, ghost), F32),
            pltpu.VMEM((half, ghost), F32),
            pltpu.VMEM((cells * width, slots), F32),
            pltpu.VMEM((CHUNK * width, slots), F32),
            pltpu.VMEM((CHUNK * width, slots), F32),
            pltpu.VMEM((2 * half, CHUNK * slots), BF16),
            pltpu.VMEM((2 * half, CHUNK * slots), BF16),
            pltpu.VMEM((2 * half, ghost), F32),
            pltpu.VMEM((steps, half, ghost), F32),
            pltpu.VMEM((steps, 2 * width, ghost), F32),
            pltpu.VMEM((steps, 2 * width, ghost), F32),
            pltpu.VMEM((cols - 1, half, ghost), F32),
            pltpu.VMEM((width * cols, LANES), F32),
            pltpu.VMEM((parts, 1, LANES), F32),
            dma((2, steps)),
            dma((2, steps)),
            dma((cols,)),
            dma((cols,)),
            dma,
            dma,
        ],
        compiler_params=pltpu.CompilerParams(
            collective_id=0, has_side_effects=True, vmem_limit_bytes=62 * 1024 * 1024
        ),
    )(
        start_block,
        stiffness,
        cell_scale.reshape(1, cells),
        node_weight.T,
        cell_count.reshape(1, 1),
        conn.T,
        send_rows,
        filter_bounds.reshape(1, 2),
    )


def solution(mesh):
    placed = (
        P("cols", "cells"),
        P(),
        P("cells"),
        P(None, "cells"),
        P("cells"),
        P(None, "cells"),
        P("cells", None),
        P(),
    )
    return jax.shard_map(
        per_device,
        mesh=mesh,
        in_specs=placed,
        out_specs=(P("cols", "cells"), P("cells", "cols"), P("cells", "cols")),
        check_vma=False,
    )
```

```python
import functools

import jax
import jax.numpy as jnp
from jax import lax
from jax.experimental import pallas as pl
from jax.experimental.pallas import tpu as pltpu
from jax.sharding import PartitionSpec as P

DEGREE = 4
MULT = 10
LANES = 128
CHUNK = 8
BF16 = jnp.bfloat16
F32 = jnp.float32
I32 = jnp.int32
MESH = pl.DeviceIdType.MESH


def iota(shape, dim):
    return lax.broadcasted_iota(I32, shape, dim)


def split(x):
    high = x.astype(BF16)
    return high, (x - high.astype(F32)).astype(BF16)


def dot(a, b):
    return jnp.dot(a, b, preferred_element_type=F32)


def dot_nt(a, b):
    return lax.dot_general(a, b, (((1,), (1,)), ((), ())), preferred_element_type=F32)


def pick(x, index):
    return jnp.take_along_axis(x, index, axis=1, mode="promise_in_bounds")


def mark(condition):
    return jnp.where(condition, 1.0, 0.0).astype(F32)


def kernel(
    cfg,
    start_hbm,
    stiff_hbm,
    scale_hbm,
    weight_hbm,
    count,
    conn_hbm,
    send_hbm,
    bounds,
    out_filtered,
    out_corr,
    out_proj,
    ordered,
    outsem,
    start,
    stiff,
    scale,
    weight,
    conn,
    send,
    insem,
    kpad,
    kk,
    newr,
    index8,
    weight8,
    scale8,
    tab,
    rows_nm,
    wt,
    sc,
    onehot,
    masks,
    vcur,
    vprev,
    xall,
    xa,
    xb,
    aa,
    ab,
    acc,
    part,
    from_left,
    from_right,
    gath,
    gsum,
    rowbuf,
    ssem,
    rsem,
    gssem,
    grsem,
    s1sem,
    r1sem,
):
    width, owned, ghost, npc, cells, parts, cols = cfg
    slots = newr.shape[1]
    groups = (owned + 2 * ghost) // ghost
    half = groups * width
    tiles = 2 * groups
    pair = 2 * width
    chunks = cells // CHUNK
    span = CHUNK * slots

    p = lax.axis_index("cells")
    q = lax.axis_index("cols")
    left = lax.rem(p + parts - 1, parts)
    right = lax.rem(p + 1, parts)
    col_peers = [lax.rem(q + d, cols) for d in range(1, cols)]

    loads = [
        pltpu.make_async_copy(source, target, insem.at[i])
        for i, (source, target) in enumerate(
            [
                (send_hbm, send),
                (conn_hbm, conn),
                (start_hbm, start),
                (scale_hbm, scale),
                (weight_hbm, weight),
                (stiff_hbm, stiff),
            ]
        )
    ]
    for load in loads:
        load.start()

    barrier = pltpu.get_barrier_semaphore()
    for other in col_peers:
        pl.semaphore_signal(barrier, inc=1, device_id=(p, other), device_id_type=MESH)

    for d in range(1, parts):
        pl.semaphore_signal(barrier, inc=1, device_id=(lax.rem(p + d, parts), q), device_id_type=MESH)

    loads[0].wait()
    lane = iota((1, LANES), 1)
    per_side = owned // 2 // LANES
    rows_nm[...] = jnp.zeros_like(rows_nm)
    places = []
    for side in range(2):
        column = jnp.broadcast_to(send[side : side + 1, :].astype(F32), (LANES, ghost)).T
        order = (iota((ghost, LANES), 0) + 1).astype(F32)
        for t in range(per_side):
            tile = side * per_side + t
            here = (iota((ghost, LANES), 1) + tile * LANES).astype(F32)
            place = jnp.sum(jnp.where(column == here, order, 0.0), axis=0, keepdims=True)
            places.append(place)
            rows_nm[tile : tile + 1, :] = mark(place == 0.0)
    free = rows_nm[...].astype(BF16)
    before = mark(iota((LANES, LANES), 0) < iota((LANES, LANES), 1)).astype(BF16)
    above = mark(iota((LANES, LANES), 0) > iota((LANES, LANES), 1)).astype(BF16)
    ones = jnp.ones((LANES, LANES), BF16)
    rank = dot(free, before) + dot(above, dot(free, ones).astype(BF16))
    base = (ghost, owned)
    for tile in range(2 * per_side):
        place = places[tile]
        shared = place + float(base[tile // per_side] - 1)
        inside = rank[tile : tile + 1, :] + float(2 * ghost)
        tab[tile : tile + 1, :] = jnp.where(place > 0.0, shared, inside).astype(I32)
    for t in range(ghost // LANES):
        a = 2 * per_side + t
        b = a + ghost // LANES
        tab[a : a + 1, :] = lane + t * LANES
        tab[b : b + 1, :] = lane + (owned + ghost + t * LANES)

    tab_cols = jnp.concatenate([tab[...], jnp.zeros((LANES - tiles, LANES), I32)], axis=0).astype(F32).T.astype(I32)
    total = jnp.zeros((2 * half, ghost), F32)
    loads[2].wait()
    for t in range(owned // LANES):
        high, low = split(start[:, t * LANES : (t + 1) * LANES])
        group = jnp.broadcast_to(tab[t : t + 1, :] >> 8, (half, LANES))
        member = mark(group == iota((half, LANES), 0) // width).astype(BF16)
        left_side = jnp.concatenate(
            [jnp.concatenate([high] * groups, axis=0) * member, jnp.concatenate([low] * groups, axis=0) * member], axis=0
        )
        column = jnp.broadcast_to(tab_cols[:, t : t + 1] & (ghost - 1), (LANES, ghost))
        total += dot(left_side, mark(column == iota((LANES, ghost), 1)).astype(BF16))
    part[0] = total[0:half] + total[half:]

    def to_left(step):
        return pltpu.make_async_remote_copy(
            src_ref=part.at[step, pl.ds(0, pair)],
            dst_ref=from_right.at[step],
            send_sem=ssem.at[0, step],
            recv_sem=rsem.at[0, step],
            device_id=(left, q),
            device_id_type=MESH,
        )

    def to_right(step):
        return pltpu.make_async_remote_copy(
            src_ref=part.at[step, pl.ds(half - pair, pair)],
            dst_ref=from_left.at[step],
            send_sem=ssem.at[1, step],
            recv_sem=rsem.at[1, step],
            device_id=(right, q),
            device_id_type=MESH,
        )

    def begin(step):
        to_left(step).start()
        to_right(step).start()

    has_left = jnp.where(p > 0, 1.0, 0.0).astype(F32)
    has_right = jnp.where(p < parts - 1, 1.0, 0.0).astype(F32)
    center = bounds[0, 0]
    inverse = 1.0 / jnp.full((1, ghost), bounds[0, 1], F32)

    def advance(step, rows, applied):
        current = vcur[rows, :]
        doubled = jnp.where(step > 1, 2.0, 1.0).astype(F32)
        first = jnp.where(step > 0, 0.0, 1.0).astype(F32)
        factor = inverse * (doubled * (1.0 - first)) + first
        following = (applied - (center * (1.0 - first)) * current) * factor - vprev[rows, :]
        vprev[rows, :] = current
        vcur[rows, :] = following

    def finish(step):
        to_left(step).wait()
        to_right(step).wait()
        a = (part[step, 0:width, :] + from_left[step, 0:width, :]) * has_left
        b = part[step, width:pair, :] + from_left[step, width:pair, :] * has_left
        advance(step, slice(0, pair), jnp.concatenate([a, b], axis=0))
        c = part[step, half - pair : half - width, :] + from_right[step, 0:width, :] * has_right
        d = (part[step, half - width : half, :] + from_right[step, width:pair, :]) * has_right
        advance(step, slice(half - pair, half), jnp.concatenate([c, d], axis=0))

    vcur[...] = jnp.zeros_like(vcur)
    vprev[...] = jnp.zeros_like(vprev)
    advance(0, slice(pair, half - pair), part[0, pair : half - pair, :])

    loads[5].wait()
    kpad[...] = jnp.zeros_like(kpad)
    kpad[0:npc, 0:npc] = stiff[...]
    k_high, k_low = split(kpad[...].T)
    kk[0:slots, :] = k_high
    kk[slots : 2 * slots, :] = k_high
    kk[2 * slots :, :] = k_low

    loads[1].wait()
    newr[...] = jnp.zeros_like(newr)
    newr[:, 0:npc] = conn[...]
    for l in range(slots // LANES):
        index = newr[:, l * LANES : (l + 1) * LANES]
        low = index & (LANES - 1)
        tile = index >> 7
        value = None
        for t in range(tiles):
            got = pick(jnp.broadcast_to(tab[t : t + 1, :], (cells, LANES)), low)
            value = got if value is None else jnp.where(tile == t, got, value)
        newr[:, l * LANES : (l + 1) * LANES] = value

    live = mark(iota((cells, slots), 0) < count[0, 0]) * (1.0 / MULT)
    loads[3].wait()
    loads[4].wait()
    wt[...] = jnp.zeros_like(wt)
    wt[:, 0:npc] = weight[...]
    wt[...] = wt[...] * live
    scale_row = jnp.concatenate([scale[...], jnp.zeros((1, LANES - cells), F32)], axis=1)
    scale_col = jnp.broadcast_to(scale_row, (LANES, LANES)).T
    sc[...] = jnp.concatenate([scale_col[0:cells]] * (slots // LANES), axis=1) * live

    @pl.loop(0, cells)
    def _(c):
        index = newr[pl.ds(c, 1), :]
        rows = pl.ds(pl.multiple_of(c * 8, 8), 8)
        index8[rows, :] = jnp.broadcast_to(index, (8, slots))
        weight8[rows, :] = jnp.broadcast_to(wt[pl.ds(c, 1), :], (8, slots))
        scale8[rows, :] = jnp.broadcast_to(sc[pl.ds(c, 1), :], (8, slots))
        place = (index & (ghost - 1)).astype(F32).astype(BF16)
        hit = jnp.broadcast_to(place, (ghost, slots)) == iota((ghost, slots), 0).astype(F32).astype(BF16)
        onehot[:, pl.ds(pl.multiple_of(c * slots, LANES), slots)] = jnp.where(
            hit, jnp.ones((), BF16), jnp.zeros((), BF16)
        )
        group = (index >> 8).astype(F32).astype(BF16)
        member = jnp.broadcast_to(group, (half, slots)) == (iota((half, slots), 0) // width).astype(F32).astype(BF16)
        masks[pl.ds(pl.multiple_of(c * half, half), half), :] = jnp.where(
            member, jnp.ones((), BF16), jnp.zeros((), BF16)
        )

    pl.semaphore_wait(barrier, parts + cols - 2)
    begin(0)

    inner_tiles = range(4, tiles - 4)
    outer_tiles = list(range(4)) + list(range(tiles - 4, tiles))

    def twice(x):
        return jnp.concatenate([x, x], axis=0)

    def collect(cell, group, which, value):
        index = twice(index8[pl.ds(pl.multiple_of(cell * 8, 8), 8), group * LANES : (group + 1) * LANES])
        low = index & (LANES - 1)
        tile = index >> 7
        for t in which:
            source = vcur[(t // 2) * width : (t // 2 + 1) * width, (t % 2) * LANES : (t % 2 + 1) * LANES]
            value = jnp.where(tile == t, pick(source, low), value)
        return value

    def rows_of(cell):
        return pl.ds(pl.multiple_of(cell * width, width), width)

    turns = chunks // 2 - 1
    late = 6 * turns
    early = cells - late

    def gather_inner(first, number):
        for c in range(number):
            cell = first + c
            for l in range(slots // LANES):
                value = collect(cell, l, inner_tiles, jnp.zeros((width, LANES), F32))
                xall[rows_of(cell), l * LANES : (l + 1) * LANES] = value

    def gather_outer(chunk, x):
        for c in range(CHUNK):
            cell = chunk * CHUNK + c
            for l in range(slots // LANES):
                cut = slice(l * LANES, (l + 1) * LANES)
                x[c * width : (c + 1) * width, cut] = collect(cell, l, outer_tiles, xall[rows_of(cell), cut])

    def spread(chunk, x, a):
        local = x[...]
        high, low = split(local)
        wide = dot(jnp.concatenate([high, low, high], axis=1), kk[...])
        for c in range(CHUNK):
            cell = chunk * CHUNK + c
            rows = slice(c * width, (c + 1) * width)
            eight = pl.ds(pl.multiple_of(cell * 8, 8), 8)
            term = wide[rows] * twice(scale8[eight, :]) + local[rows] * twice(weight8[eight, :])
            high, low = split(term)
            for g in range(groups):
                member = masks[pl.ds(pl.multiple_of(cell * half + g * width, width), width), :]
                a[g * width : (g + 1) * width, c * slots : (c + 1) * slots] = high * member
                a[half + g * width : half + (g + 1) * width, c * slots : (c + 1) * slots] = low * member

    def scatter(chunk, a):
        acc[...] += dot_nt(a[...], onehot[:, pl.ds(pl.multiple_of(chunk * span, LANES), span)])

    def gather_copy(d):
        return pltpu.make_async_remote_copy(
            src_ref=vcur,
            dst_ref=gath.at[d - 1],
            send_sem=gssem.at[d],
            recv_sem=grsem.at[d],
            device_id=(p, col_peers[d - 1]),
            device_id_type=MESH,
        )

    last = DEGREE + 1

    @pl.loop(1, last + 1)
    def _(step):
        @pl.loop(0, early // 23)
        def _(i):
            gather_inner(i * 23, 23)

        finish(step - 1)

        @pl.when(step == last)
        def _():
            for d in range(1, cols):
                gather_copy(d).start()

        acc[...] = jnp.zeros_like(acc)
        gather_outer(0, xa)
        gather_outer(1, xb)
        spread(0, xa, aa)

        @pl.loop(0, chunks // 2 - 1)
        def _(i):
            n = 2 * i
            gather_inner(early + 6 * i, 6)
            spread(n + 1, xb, ab)
            gather_outer(n + 2, xa)
            scatter(n, aa)
            spread(n + 2, xa, aa)
            gather_outer(n + 3, xb)
            scatter(n + 1, ab)

        spread(chunks - 1, xb, ab)
        scatter(chunks - 2, aa)
        scatter(chunks - 1, ab)
        part[step] = acc[0:half, :] + acc[half:, :]

        @pl.when(step < last)
        def _():
            begin(step)
            advance(step, slice(pair, half - pair), part[step, pair : half - pair, :])

    for d in range(1, cols):
        gather_copy(d).wait()

    gram = jnp.zeros((cols * width, 2 * width), F32)
    for g in range(groups):
        rows = slice(g * width, (g + 1) * width)
        mine = part[last, rows, :]
        if 0 < g < groups - 1:
            mine = jnp.concatenate([vcur[rows, :], mine], axis=0)
        else:
            mine = jnp.concatenate([jnp.zeros_like(mine), mine], axis=0)
        all_rows = jnp.concatenate([vcur[rows, :]] + [gath[d, rows, :] for d in range(cols - 1)], axis=0)
        mine_high, mine_low = split(mine)
        all_high, all_low = split(all_rows)
        gram += dot_nt(all_high, mine_high) + dot_nt(all_high, mine_low) + dot_nt(all_low, mine_high)
    gram = gram * (1.0 / (parts * owned))
    gsum[...] = jnp.zeros_like(gsum)
    for d in range(cols):
        group = lax.rem(q + cols - d, cols)
        gsum[pl.ds(pl.multiple_of(group * width, width), width), 0 : 2 * width] = gram[d * width : (d + 1) * width]

    def row_copy(d):
        return pltpu.make_async_remote_copy(
            src_ref=gsum.at[pl.ds(lax.rem(p + d, parts), 1)],
            dst_ref=rowbuf.at[d],
            send_sem=s1sem,
            recv_sem=r1sem,
            device_id=(lax.rem(p + d, parts), q),
            device_id_type=MESH,
        )

    middle = parts // 2
    row_copy(middle).start()

    @pl.loop(1, middle)
    def _(j):
        row_copy(middle - j).start()
        row_copy(middle + j).start()

    rowbuf[0] = gsum[pl.ds(p, 1), :]

    for t in range(owned // LANES):
        index = jnp.broadcast_to(tab[t : t + 1, :], (width, LANES))
        low = index & (LANES - 1)
        tile = index >> 7
        value = None
        for s in range(2, tiles - 2):
            source = vcur[(s // 2) * width : (s // 2 + 1) * width, (s % 2) * LANES : (s % 2 + 1) * LANES]
            got = pick(source, low)
            value = got if value is None else jnp.where(tile == s, got, value)
        ordered[:, t * LANES : (t + 1) * LANES] = value
    store = pltpu.make_async_copy(ordered, out_filtered, outsem)
    store.start()

    every = pltpu.make_async_remote_copy(
        src_ref=rowbuf.at[pl.ds(1, parts - 1)],
        dst_ref=rowbuf.at[pl.ds(1, parts - 1)],
        send_sem=s1sem,
        recv_sem=r1sem,
        device_id=(right, q),
        device_id_type=MESH,
    )
    store.wait()
    every.wait_send()
    every.wait_recv()
    row = jnp.sum(rowbuf[...], axis=0)
    out_corr[...] = row[:, 0:width]
    out_proj[...] = row[:, width : 2 * width]


def per_device(
    start_block, stiffness, cell_scale, node_weight, cell_count, conn, send_rows, filter_bounds
):
    width, owned = start_block.shape
    ghost = send_rows.shape[1]
    npc, cells = conn.shape
    parts = lax.axis_size("cells")
    cols = lax.axis_size("cols")
    slots = -(-npc // LANES) * LANES
    half = (owned + 2 * ghost) // ghost * width
    steps = DEGREE + 2
    cfg = (width, owned, ghost, npc, cells, parts, cols)
    vmem = pl.BlockSpec(memory_space=pltpu.VMEM)
    hbm = pl.BlockSpec(memory_space=pltpu.HBM)
    smem = pl.BlockSpec(memory_space=pltpu.SMEM)
    dma = pltpu.SemaphoreType.DMA
    rows = cols * width // parts
    return pl.pallas_call(
        functools.partial(kernel, cfg),
        out_shape=(
            jax.ShapeDtypeStruct((width, owned), F32),
            jax.ShapeDtypeStruct((rows, width), F32),
            jax.ShapeDtypeStruct((rows, width), F32),
        ),
        in_specs=[hbm, hbm, hbm, hbm, smem, hbm, hbm, smem],
        out_specs=(hbm, vmem, vmem),
        scratch_shapes=[
            pltpu.VMEM((width, owned), F32),
            dma,
            pltpu.VMEM((width, owned), F32),
            pltpu.VMEM((npc, npc), F32),
            pltpu.VMEM((1, cells), F32),
            pltpu.VMEM((cells, npc), F32),
            pltpu.VMEM((cells, npc), I32),
            pltpu.VMEM((2, ghost), I32),
            dma((6,)),
            pltpu.VMEM((slots, slots), F32),
            pltpu.VMEM((3 * slots, slots), BF16),
            pltpu.VMEM((cells, slots), I32),
            pltpu.VMEM((cells * 8, slots), I32),
            pltpu.VMEM((cells * 8, slots), F32),
            pltpu.VMEM((cells * 8, slots), F32),
            pltpu.VMEM((16, LANES), I32),
            pltpu.VMEM((LANES, LANES), F32),
            pltpu.VMEM((cells, slots), F32),
            pltpu.VMEM((cells, slots), F32),
            pltpu.VMEM((ghost, cells * slots), BF16),
            pltpu.VMEM((cells * half, slots), BF16),
            pltpu.VMEM((half, ghost), F32),
            pltpu.VMEM((half, ghost), F32),
            pltpu.VMEM((cells * width, slots), F32),
            pltpu.VMEM((CHUNK * width, slots), F32),
            pltpu.VMEM((CHUNK * width, slots), F32),
            pltpu.VMEM((2 * half, CHUNK * slots), BF16),
            pltpu.VMEM((2 * half, CHUNK * slots), BF16),
            pltpu.VMEM((2 * half, ghost), F32),
            pltpu.VMEM((steps, half, ghost), F32),
            pltpu.VMEM((steps, 2 * width, ghost), F32),
            pltpu.VMEM((steps, 2 * width, ghost), F32),
            pltpu.VMEM((cols - 1, half, ghost), F32),
            pltpu.VMEM((width * cols, LANES), F32),
            pltpu.VMEM((parts, 1, LANES), F32),
            dma((2, steps)),
            dma((2, steps)),
            dma((cols,)),
            dma((cols,)),
            dma,
            dma,
        ],
        compiler_params=pltpu.CompilerParams(
            collective_id=0, has_side_effects=True, vmem_limit_bytes=62 * 1024 * 1024
        ),
    )(
        start_block,
        stiffness,
        cell_scale.reshape(1, cells),
        node_weight.T,
        cell_count.reshape(1, 1),
        conn.T,
        send_rows,
        filter_bounds.reshape(1, 2),
    )


def solution(mesh):
    placed = (
        P("cols", "cells"),
        P(),
        P("cells"),
        P(None, "cells"),
        P("cells"),
        P(None, "cells"),
        P("cells", None),
        P(),
    )
    return jax.shard_map(
        per_device,
        mesh=mesh,
        in_specs=placed,
        out_specs=(P("cols", "cells"), P("cells", "cols"), P("cells", "cols")),
        check_vma=False,
    )
```
